256 devices in a mesh: blk: 128 (over z, x_lo, y, core), rep: 2 (over x_hi).
Axes of the slice: x: 4 (x_hi: 2, x_lo: 2; x = x_hi * 2 + x_lo), y: 4, z: 8, core: 2. Of those that a mesh axis runs over, the one named last changes fastest.
Arguments:
- saved_rows: float32 [131072, 400], P('blk'), may hold values from -1.8 to 1.8
- saved_state: float32 [131072], P('blk'), may hold values from 0.001 to 0.1
- old_starts: int32 [64], replicated, may hold values from 0 to 121087, as said below
- new_starts: int32 [128], replicated, may hold values from 0 to 121920, as said below
- relations: float32 [4131, 400], replicated, may hold values from -3.6 to 3.6
- source_rows: int32 [128, 4, 2, 1000], P('blk'), may hold values from 0 to 896
- target_rows: int32 [128, 4, 2, 1000], P('blk'), may hold values from 0 to 896
- relation_ids: int32 [128, 4, 2, 1000], P('blk'), may hold values from 0 to 4130
- negative_rows: int32 [128, 4, 2, 512], P('blk'), may hold values from 0 to 896
- live_groups: int32 [128, 4], P('blk'), may hold values from 1 to 2
Outputs:
- embeddings: float32 [131072, 400], P(('blk', 'rep'))
- adagrad_state: float32 [131072], P(('blk', 'rep'))
The draws below stay inside these ranges and needn't reach their ends.
Inputs may be any that keep to these rules, and one draw needn't show every extreme that they name: new_starts[q] = q * 960 + an offset of 0 to 63, and 0 for q = 0 and for the last q; where q * 64 is a multiple of 128, the offset is smaller than the offset of saved partition q * 64 / 128; the last partition ends at entity 122880. old_starts[p] = p * 1920 + an offset of 1 to 127; the offset of partition 0 is 0 and that of the last is 127; the last saved partition ends at entity 122880.
All inputs are finite; a program needn't handle non-finite values.
Results may differ from the reference program's by a relative error of at most 0.00031.
Values sent between devices are 32-bit elements; how exact they have to be, the bound alone decides.
A program may use at most 128 MiB of HBM per device.

```python
import math
import jax
import jax.numpy as jnp
from jax import lax

D = 400
NREL = 4131
CAP = 1024
STEPS = 4
C = 1000
NEG = 512
GROUPS = 2
JITTER = 64
PART_ROWS = 960
ENTITIES = 122880
OLD_CAP = 2048
OLD_JITTER = 128
OLD_ROWS = 1920
SAVED = 131072
N_BLK = 128


def saved_offsets(key):
    inner = jax.random.fold_in(key, 23)
    offsets = jax.random.randint(inner, (64,), 1, OLD_JITTER)
    return offsets.at[0].set(0).at[63].set(OLD_JITTER - 1)


def draw_old_starts(key, part):
    offsets = saved_offsets(key)
    return (jnp.arange(64) * OLD_ROWS + offsets).astype(jnp.int32)


def draw_new_starts(key, part):
    shared = saved_offsets(key)
    key = jax.random.fold_in(key, 11)
    count = ENTITIES // PART_ROWS
    index_q = jnp.arange(count)
    aligned = index_q * 64 % count == 0
    matched = jnp.minimum(index_q * 64 // count, 63)
    bound = jnp.where(aligned, jnp.minimum(shared[matched], JITTER), JITTER)
    bound = jnp.maximum(bound, 1)
    offsets = jax.random.randint(key, (count,), 0, bound)
    offsets = offsets.at[0].set(0).at[count - 1].set(0)
    return (index_q * PART_ROWS + offsets).astype(jnp.int32)


def with_ends(result, rng, least, top_value):
    index_at = [jax.random.randint(jax.random.fold_in(rng, axis), (), 0, length) for axis, length in enumerate(result.shape)]
    longest = result.shape.index(max(result.shape))
    next_to = index_at[:longest] + [(index_at[longest] + 1) % result.shape[longest]] + index_at[longest + 1:]
    return result.at[tuple(index_at)].set(least).at[tuple(next_to)].set(top_value)


def steps_of(own_key, shape, shards, low, largest):
    factor_of = 1.0
    for dim, shards_of in shards:
        steps = jax.random.uniform(jax.random.fold_in(jax.random.fold_in(own_key, 6), dim), (shards_of,), jnp.float32, low / len(shards), largest / len(shards))
        factor_of = factor_of * jnp.repeat(jnp.exp(steps), shape[dim] // shards_of).reshape((-1,) + (1,) * (len(shape) - 1 - dim))
    return factor_of


def gaussian(own_key, dims, deviation, most, cuts=(), held_as=jnp.bfloat16):
    values = deviation * jax.random.normal(own_key, dims, jnp.float32)
    if cuts:
        values = values * steps_of(own_key, dims, cuts, -0.22, 0.18)
    return jnp.clip(values, -most, most).astype(held_as)


def setup_inputs(seed: int = 0) -> dict:
    key_list = jax.random.split(jax.random.key(seed), 11)
    return {
        "saved_rows": gaussian(key_list[0], (SAVED, D), 0.3, 1.8, ((0, 128),), jnp.float32),
        "saved_state": jnp.clip(jnp.exp(math.log(0.1) - 4.6051702 * jax.random.uniform(key_list[1], (SAVED,), jnp.float32) ** steps_of(key_list[1], (SAVED,), ((0, 128),), -0.2, 0.2)), 0.001, 0.1),
        "old_starts": draw_old_starts(jax.random.fold_in(key_list[10], 71), 0),
        "new_starts": draw_new_starts(jax.random.fold_in(key_list[10], 71), 0),
        "relations": gaussian(key_list[4], (NREL, D), 0.6, 3.6, (), jnp.float32),
        "source_rows": with_ends(jax.random.randint(key_list[5], (N_BLK, STEPS, GROUPS, C), 0, CAP - 2 * (CAP // 16) + 1), jax.random.fold_in(key_list[5], 1), 0, (CAP - 2 * (CAP // 16) + 1) - 1).astype(jnp.int32),
        "target_rows": with_ends(jax.random.randint(key_list[6], (N_BLK, STEPS, GROUPS, C), 0, CAP - 2 * (CAP // 16) + 1), jax.random.fold_in(key_list[6], 1), 0, (CAP - 2 * (CAP // 16) + 1) - 1).astype(jnp.int32),
        "relation_ids": with_ends(jax.random.randint(key_list[7], (N_BLK, STEPS, GROUPS, C), 0, NREL), jax.random.fold_in(key_list[7], 1), 0, NREL - 1).astype(jnp.int32),
        "negative_rows": with_ends(jax.random.randint(key_list[8], (N_BLK, STEPS, GROUPS, NEG), 0, CAP - 2 * (CAP // 16) + 1), jax.random.fold_in(key_list[8], 1), 0, (CAP - 2 * (CAP // 16) + 1) - 1).astype(jnp.int32),
        "live_groups": with_ends(jax.random.randint(key_list[9], (N_BLK, STEPS), 1, GROUPS + 1), jax.random.fold_in(key_list[9], 1), 1, GROUPS).astype(jnp.int32),
    }


LR_RATE = 0.2
EPSILON = 1e-10

def restore_table(saved_rows, saved_state, old_starts, new_starts):
    ends = jnp.concatenate([new_starts[1:], jnp.array([ENTITIES], jnp.int32)])
    slot_ids = jnp.arange(CAP, dtype=jnp.int32)
    entity_ids = new_starts[:, None] + slot_ids[None, :]
    valid = slot_ids[None, :] < (ends - new_starts)[:, None]
    partition = lax.optimization_barrier(jnp.sum((old_starts[None, None, :] <= entity_ids[:, :, None]).astype(jnp.int32), axis=2)) - 1
    partition = jnp.clip(partition, 0, old_starts.shape[0] - 1).astype(jnp.int32)
    source_slot = partition * OLD_CAP + entity_ids - old_starts[partition]
    source_slot = jnp.where(valid, source_slot, 0).astype(jnp.int32)
    restored = jnp.where(valid[:, :, None], saved_rows[source_slot], jnp.float32(0.0))
    state = jnp.where(valid, saved_state[source_slot], jnp.float32(1.0))
    return (restored, state)

def group_grads(left_table, right_table, relations, sources, targets, rel_index, negatives):
    half_width = left_table.shape[1] // 2
    src_emb = left_table[sources]
    dst_emb = right_table[targets]
    rel_emb = relations[rel_index]
    neg_emb = right_table[negatives]
    s_re, s_im = (src_emb[:, :half_width], src_emb[:, half_width:])
    r_re, r_im = (rel_emb[:, :half_width], rel_emb[:, half_width:])
    query = jnp.concatenate([s_re * r_re - s_im * r_im, s_re * r_im + s_im * r_re], axis=1)
    positive = lax.optimization_barrier(jnp.sum(query * dst_emb, axis=1))
    query_b = query.astype(jnp.bfloat16)
    neg_b = neg_emb.astype(jnp.bfloat16)
    scores = lax.dot_general(query_b.astype(jnp.float32), neg_b.astype(jnp.float32), (((1,), (1,)), ((), ())))
    dpos = -jax.nn.sigmoid(-positive)
    dneg = (jax.nn.sigmoid(scores) / negatives.shape[0]).astype(jnp.bfloat16)
    grad_query = dpos[:, None] * dst_emb + jnp.dot(dneg.astype(jnp.float32), neg_b.astype(jnp.float32))
    grad_neg = lax.dot_general(dneg.astype(jnp.float32), query_b.astype(jnp.float32), (((0,), (0,)), ((), ())))
    grad_dst = dpos[:, None] * query
    gq_re, gq_im = (grad_query[:, :half_width], grad_query[:, half_width:])
    grad_src = jnp.concatenate([gq_re * r_re + gq_im * r_im, gq_im * r_re - gq_re * r_im], axis=1)
    left_grad = jnp.zeros(left_table.shape, jnp.float32).at[sources].add(grad_src)
    right_grad = jnp.zeros(right_table.shape, jnp.float32).at[targets].add(grad_dst).at[negatives].add(grad_neg)
    return (left_grad, right_grad)

def reference(saved_rows, saved_state, old_starts, new_starts, relations, source_rows, target_rows, relation_ids, negative_rows, live_groups):
    restored, state = restore_table(saved_rows, saved_state, old_starts, new_starts)
    left_rows = restored
    carried = jnp.zeros(restored.shape, jnp.float32)
    batched = jax.vmap(group_grads, in_axes=(0, 0, None, 0, 0, 0, 0))
    for step_index in range(STEPS):
        right_rows = jnp.roll(restored, step_index, axis=0)
        left_grad = jnp.zeros(restored.shape, jnp.float32)
        right_grad = jnp.zeros(restored.shape, jnp.float32)
        for group_index in range(GROUPS):
            grad_a, grad_b = batched(left_rows, right_rows, relations, source_rows[:, step_index, group_index], target_rows[:, step_index, group_index], relation_ids[:, step_index, group_index], negative_rows[:, step_index, group_index])
            live_mask = (group_index < live_groups[:, step_index]).astype(jnp.float32)[:, None, None]
            left_grad = left_grad + grad_a * live_mask
            right_grad = right_grad + grad_b * live_mask
        carried = carried + jnp.roll(right_grad, -step_index, axis=0)
        state = state + lax.optimization_barrier(jnp.mean(left_grad * left_grad, axis=2))
        left_rows = left_rows - LR_RATE * left_grad / (jnp.sqrt(state)[:, :, None] + EPSILON)
    state = state + lax.optimization_barrier(jnp.mean(carried * carried, axis=2))
    final_rows = left_rows - LR_RATE * carried / (jnp.sqrt(state)[:, :, None] + EPSILON)
    return (final_rows.reshape(N_BLK * CAP, D), state.reshape(N_BLK * CAP))
```

```python
import functools

import jax
import jax.numpy as jnp
from jax import lax
from jax.experimental import pallas as pl
from jax.experimental.pallas import tpu as pltpu
from jax.sharding import PartitionSpec as P

LR = 0.2
EPS = 1e-10
F32 = jnp.float32
BF = jnp.bfloat16
D = 400
H = 200
CAP = 1024
HALF = 512
E = 1024
N = 512
CH = 512
LOW = 192
OLD_CAP = 2048
ENTITIES = 122880
STEPS = 4
MESH = pl.DeviceIdType.MESH
ROWS_W = 512
VMEM_LIMIT = 62 * 1024 * 1024
NT = (((1,), (1,)), ((), ()))
NN = (((1,), (0,)), ((), ()))
BOTH = ("blk", "rep")
VMEM = pl.BlockSpec(memory_space=pltpu.VMEM)
ANY = pl.BlockSpec(memory_space=pl.ANY)
SMEM = pl.BlockSpec(memory_space=pltpu.SMEM)


def dot(a, b, dims):
    return lax.dot_general(a, b, dims, preferred_element_type=F32)


def split_to(ref, col, x):
    hi = x.astype(BF)
    ref[0:D, col] = hi
    ref[D : 2 * D, col] = (x - hi.astype(F32)).astype(BF)


def remote(src, dst, send, recv, device):
    return pltpu.make_async_remote_copy(
        src_ref=src, dst_ref=dst, send_sem=send, recv_sem=recv, device_id=device,
        device_id_type=MESH)


def train_kernel(blocks, ids, idx, own, own_state, rel, out, out_state,
                 tab, st, rel_s, rel_t, rows, left, state, lhl, rhl, ohs, oht, gshl, gdhl,
                 q_s, g_s, qb_s, dn_s, glo, gli, gro, gri, gsum, carr, lfin, sfin,
                 local_sem, tab_send, tab_recv, gl_send, gl_recv, gr_send, gr_recv,
                 home_send, home_recv, fin_send, fin_recv):
    b = lax.axis_index("blk")
    r = lax.axis_index("rep")
    c = lax.rem(b, 2)
    m2 = b - c
    sibling = (m2 + 1 - c, r)
    ahead = (lax.rem(b + 2, blocks), r)
    behind = (lax.rem(b + blocks - 2, blocks), r)
    here = c == r
    mine = pl.ds(pl.multiple_of(c * HALF, HALF), HALF)
    theirs = pl.ds(pl.multiple_of((1 - c) * HALF, HALF), HALF)

    def home(s):
        return (lax.rem(m2 + r - s + blocks, blocks), c)

    def origin(s):
        i = lax.rem(b + s, blocks)
        odd = lax.rem(i, 2)
        return (i - odd + r, odd)

    get_rel = pltpu.make_async_copy(rel, rel_s, local_sem.at[0])
    get_own = pltpu.make_async_copy(own, tab.at[0], local_sem.at[1])
    get_state = pltpu.make_async_copy(own_state, st.at[0], local_sem.at[2])
    get_own.start()
    get_state.start()
    get_rel.start()

    barrier = pltpu.get_barrier_semaphore()
    pl.semaphore_signal(barrier, inc=1, device_id=sibling, device_id_type=MESH)
    pl.semaphore_signal(barrier, inc=1, device_id=behind, device_id_type=MESH)
    for s in range(1, STEPS):
        pl.semaphore_signal(barrier, inc=1, device_id=origin(s), device_id_type=MESH)

    @pl.when(jnp.logical_not(here))
    def _():
        pl.semaphore_signal(barrier, inc=1, device_id=origin(0), device_id_type=MESH)

    pl.semaphore_wait(barrier, STEPS + 2 - here.astype(jnp.int32))

    share = remote(tab.at[0], tab.at[1], tab_send.at[0], tab_recv.at[0], sibling)
    share_state = remote(st.at[0], st.at[1], tab_send.at[1], tab_recv.at[1], sibling)
    onward = remote(tab.at[0], tab.at[2], tab_send.at[2], tab_recv.at[2], ahead)
    share_on = remote(tab.at[2], tab.at[3], tab_send.at[3], tab_recv.at[3], sibling)
    far = remote(tab.at[3 - c, :, mine], tab.at[4, :, mine], tab_send.at[4], tab_recv.at[4], ahead)
    share_far = remote(tab.at[4, :, mine], tab.at[4, :, mine], tab_send.at[5], tab_recv.at[5], sibling)
    share_far_in = remote(tab.at[4, :, theirs], tab.at[4, :, theirs], tab_send.at[5], tab_recv.at[5], sibling)

    def gl_copy(s, k):
        p = lax.rem(s, 2)
        part = theirs if k == 0 else mine
        return remote(glo.at[p, :, part], gli.at[p, :, part], gl_send.at[p, k], gl_recv.at[p, k], sibling)

    def gr_copy(s):
        p = lax.rem(s, 2)
        return remote(gro.at[p], gri.at[p], gr_send.at[p], gr_recv.at[p], sibling)

    def home_copy(s):
        p = lax.rem(s, 2)
        return remote(gsum.at[p], carr.at[s], home_send.at[p], home_recv.at[s], home(s))

    def home_local(s):
        return pltpu.make_async_copy(gsum.at[0], carr.at[0], local_sem.at[3])

    get_own.wait()
    get_state.wait()
    share.start()
    share_state.start()

    @pl.when(c == 1)
    def _():
        onward.start()

    get_rel.wait()

    def gather(s):
        def body(k, carry):
            base = pl.multiple_of(k * 128, 128)
            for i in range(128):
                rows[i : i + 1, 0:D] = rel_s[pl.ds(ids[s, base + i], 1), :]
            rel_t[:, pl.ds(base, 128)] = rows[...].T[0:D]
            return carry

        lax.fori_loop(0, E // 128, body, 0)

    gather(0)
    share.wait_recv()
    share_state.wait_recv()
    state[...] = jnp.where(here, st[0], st[1])
    for c0 in range(0, CAP, 256):
        col = pl.ds(c0, 256)
        x = jnp.where(here, tab[0, :, col], tab[1, :, col])
        left[:, col] = x
        split_to(lhl, col, x)

    def bucket(s, carry):
        p = lax.rem(s, 2)
        same = jnp.where(here, 0, 1)
        slot = jnp.where(
            s == 0, same,
            jnp.where(
                s == 1, jnp.where(r == 0, 3 - c, c),
                jnp.where(s == 2, 2 + same, jnp.where(r == 0, 4, 2 + c))))
        for c0 in range(0, CAP, 256):
            col = pl.ds(c0, 256)
            split_to(rhl, col, tab[slot, :, col])
        row_n = lax.broadcasted_iota(jnp.int32, (CAP, N), 0)
        ohn = jnp.where(row_n == idx[s, 2:3, 0:N], 1.0, 0.0).astype(BF)
        oht[:, E : E + N] = ohn
        nbt = dot(rhl[0:D, :], ohn, NN).astype(BF)
        nb = nbt.T
        for e in range(E // CH):
            col = pl.ds(e * CH, CH)
            live = idx[s, 4:5, col].astype(F32)
            row = lax.broadcasted_iota(jnp.int32, (CAP, CH), 0)
            oh_s = jnp.where(row == idx[s, 0:1, col], 1.0, 0.0).astype(BF)
            ohs[:, col] = oh_s
            sh = dot(lhl[...], oh_s, NN)
            oh_t = jnp.where(row == idx[s, 1:2, col], 1.0, 0.0).astype(BF)
            oht[:, col] = oh_t
            dh = dot(rhl[...], oh_t, NN)
            d = dh[0:D] + dh[D : 2 * D]
            s_re = sh[0:H] + sh[D : D + H]
            s_im = sh[H:D] + sh[D + H : 2 * D]
            r_re = rel_t[0:H, col]
            r_im = rel_t[H:D, col]
            q_s[0:H, :] = s_re * r_re - s_im * r_im
            q_s[H:D, :] = s_re * r_im + s_im * r_re
            q = q_s[...]
            pos = jnp.sum(q * d, axis=0, keepdims=True)
            dpos = -jax.nn.sigmoid(-pos) * live
            split_to(gdhl, col, dpos * q)
            qb = q.astype(BF)
            qb_s[:, col] = qb
            scores = dot(nb, qb, NN)
            dneg = (jax.nn.sigmoid(scores) * (live * (1.0 / N))).astype(BF)
            dn_s[:, col] = dneg
            g_s[...] = dpos * d + dot(nbt, dneg, NN)
            g_re = g_s[0:H, :]
            g_im = g_s[H:D, :]
            q_s[0:H, :] = g_re * r_re + g_im * r_im
            q_s[H:D, :] = g_im * r_re - g_re * r_im
            split_to(gshl, col, q_s[...])
        split_to(gdhl, pl.ds(E, N), dot(qb_s[...], dn_s[...], NT))

        def right_half(part):
            y = dot(gdhl[...], oht[part, :], NT)
            return y[0:D] + y[D : 2 * D]

        def left_half(part):
            y = dot(gshl[...], ohs[part, :], NT)
            glo[p, :, part] = y[0:D] + y[D : 2 * D]

        gro[p] = right_half(theirs)
        gr_copy(s).start()
        gsum[p] = right_half(mine)
        left_half(theirs)
        gl_copy(s, 0).start()
        gr_copy(s).wait()
        gsum[p] = gsum[p] + gri[p]

        @pl.when(jnp.logical_and(s == 0, here))
        def _():
            home_local(s).start()

        @pl.when(jnp.logical_or(s > 0, jnp.logical_not(here)))
        def _():
            home_copy(s).start()

        left_half(mine)

        @pl.when(s < STEPS - 1)
        def _():
            gl_copy(s, 1).start()
            gather(s + 1)

        @pl.when(s == 0)
        def _():
            @pl.when(c == 0)
            def _():
                onward.start()
                share_on.wait_recv()

            @pl.when(c == 1)
            def _():
                onward.wait_recv()
                share_on.start()

        @pl.when(s == 1)
        def _():
            @pl.when(r == 0)
            def _():
                far.start()

            @pl.when(c == 0)
            def _():
                onward.wait_recv()
                share_on.start()

            @pl.when(c == 1)
            def _():
                share_on.wait_recv()

        @pl.when(jnp.logical_and(s == 2, r == 0))
        def _():
            far.wait_recv()
            share_far.start()
            share_far_in.wait_recv()

        @pl.when(jnp.logical_and(s == 1, here))
        def _():
            home_local(s).wait()

        @pl.when(jnp.logical_and(s == 1, jnp.logical_not(here)))
        def _():
            home_copy(0).wait_send()

        @pl.when(s > 1)
        def _():
            home_copy(s - 1).wait_send()

        gl_copy(s, 0).wait_send()
        gl_in = remote(glo.at[p, :, mine], gli.at[p, :, mine], gl_send.at[p, 0], gl_recv.at[p, 0], sibling)
        gl_in.wait_recv()

        @pl.when(s < STEPS - 1)
        def _():
            gl_copy(s, 1).wait_send()
            other = remote(glo.at[p, :, theirs], gli.at[p, :, theirs], gl_send.at[p, 1], gl_recv.at[p, 1], sibling)
            other.wait_recv()
            for c0 in range(0, CAP, 256):
                col = pl.ds(c0, 256)
                g = glo[p, :, col] + gli[p, :, col]
                v = state[:, col] + jnp.sum(g * g, axis=0, keepdims=True) * (1.0 / D)
                x = left[:, col] - LR * g / (jnp.sqrt(v[0:1]) + EPS)
                state[:, col] = v
                left[:, col] = x
                split_to(lhl, col, x)

        return carry

    lax.fori_loop(0, STEPS, bucket, 0)

    p = (STEPS - 1) % 2
    g = glo[p, :, mine] + gli[p, :, mine]
    v = state[:, mine] + jnp.sum(g * g, axis=0, keepdims=True) * (1.0 / D)
    lfin[0] = left[:, mine] - LR * g / (jnp.sqrt(v[0:1]) + EPS)
    sfin[0] = v
    fin = remote(lfin.at[0], lfin.at[1], fin_send.at[0], fin_recv.at[0], home(0))
    fin_state = remote(sfin.at[0], sfin.at[1], fin_send.at[1], fin_recv.at[1], home(0))
    fin_here = pltpu.make_async_copy(lfin.at[0], lfin.at[1], local_sem.at[0])
    fin_state_here = pltpu.make_async_copy(sfin.at[0], sfin.at[1], local_sem.at[1])

    @pl.when(here)
    def _():
        fin_here.start()
        fin_state_here.start()

    @pl.when(jnp.logical_not(here))
    def _():
        fin.start()
        fin_state.start()
        home_copy(0).wait_recv()

    share.wait_send()
    share_state.wait_send()
    onward.wait_send()
    share_on.wait_send()

    @pl.when(r == 0)
    def _():
        far.wait_send()
        share_far.wait_send()

    for s in range(1, STEPS):
        home_copy(s).wait_recv()
    total = (carr[0] + carr[1]) + (carr[2] + carr[3])

    @pl.when(here)
    def _():
        fin_here.wait()
        fin_state_here.wait()

    @pl.when(jnp.logical_not(here))
    def _():
        fin.wait()
        fin_state.wait()

    v = sfin[1] + jnp.sum(total * total, axis=0, keepdims=True) * (1.0 / D)
    out[...] = lfin[1] - LR * total / (jnp.sqrt(v[0:1]) + EPS)
    out_state[...] = v
    home_copy(STEPS - 1).wait_send()


def train_call(blocks, ids, idx, own, own_state, rel):
    dma = pltpu.SemaphoreType.DMA
    return pl.pallas_call(
        functools.partial(train_kernel, blocks),
        out_shape=(jax.ShapeDtypeStruct((D, HALF), F32), jax.ShapeDtypeStruct((8, HALF), F32)),
        in_specs=[SMEM, VMEM, ANY, ANY, ANY],
        out_specs=(VMEM, VMEM),
        scratch_shapes=[
            pltpu.VMEM((5, D, CAP), F32),
            pltpu.VMEM((2, 8, CAP), F32),
            pltpu.VMEM(rel.shape, F32),
            pltpu.VMEM((D, E), F32),
            pltpu.VMEM((128, ROWS_W), F32),
            pltpu.VMEM((D, CAP), F32),
            pltpu.VMEM((8, CAP), F32),
            pltpu.VMEM((2 * D, CAP), BF),
            pltpu.VMEM((2 * D, CAP), BF),
            pltpu.VMEM((CAP, E), BF),
            pltpu.VMEM((CAP, E + N), BF),
            pltpu.VMEM((2 * D, E), BF),
            pltpu.VMEM((2 * D, E + N), BF),
            pltpu.VMEM((D, CH), F32),
            pltpu.VMEM((D, CH), F32),
            pltpu.VMEM((D, E), BF),
            pltpu.VMEM((N, E), BF),
            pltpu.VMEM((2, D, CAP), F32),
            pltpu.VMEM((2, D, CAP), F32),
            pltpu.VMEM((2, D, HALF), F32),
            pltpu.VMEM((2, D, HALF), F32),
            pltpu.VMEM((2, D, HALF), F32),
            pltpu.VMEM((STEPS, D, HALF), F32),
            pltpu.VMEM((2, D, HALF), F32),
            pltpu.VMEM((2, 8, HALF), F32),
            dma((4,)),
            dma((6,)),
            dma((6,)),
            dma((2, 2)),
            dma((2, 2)),
            dma((2,)),
            dma((2,)),
            dma((2,)),
            dma((STEPS,)),
            dma((2,)),
            dma((2,)),
        ],
        compiler_params=pltpu.CompilerParams(
            vmem_limit_bytes=VMEM_LIMIT, collective_id=0, has_side_effects=True),
        cost_estimate=pl.CostEstimate(flops=4 * 10**10, bytes_accessed=10**7, transcendentals=0),
        name="train",
    )(ids, idx, own, own_state, rel)


def local(blocks, saved_rows, saved_state, old_starts, new_starts, relations,
          source_rows, target_rows, relation_ids, negative_rows, live_groups):
    b = lax.axis_index("blk")
    r = lax.axis_index("rep")
    c = b % 2

    def move(x, route):
        pairs = []
        for m in range(blocks // 2):
            for rr in range(2):
                for cc in range(2):
                    to = route(m, rr, cc)
                    if to is not None:
                        tb, tr = to
                        pairs.append(((2 * m + cc) * 2 + rr, (tb % blocks) * 2 + tr))
        return lax.ppermute(x, BOTH, pairs)

    def sibling(x):
        return move(x, lambda m, rr, cc: (2 * m + 1 - cc, rr))

    def pad(x, fill=-1):
        return jnp.pad(x, ((0, 0), (0, E - x.shape[1])), constant_values=fill)[:, None]

    def pack(g):
        def one(x):
            return pad(lax.dynamic_index_in_dim(x[0], g, 1, keepdims=False))

        rels = pad(lax.dynamic_index_in_dim(relation_ids[0], g, 1, keepdims=False), 0)
        alive = (g < live_groups[0]).astype(jnp.int32)[:, None]
        alive = pad(jnp.broadcast_to(alive, (STEPS, source_rows.shape[3])), 0)
        parts = [one(source_rows), one(target_rows), one(negative_rows), rels, alive]
        return jnp.concatenate(parts + [jnp.zeros((STEPS, 3, E), jnp.int32)], axis=1)

    theirs = sibling(pack(1 - c))
    idx = jnp.where(c == r, pack(c), theirs)

    table = saved_rows.T
    last = old_starts.shape[0] - 1

    def tail_end(q):
        p = q // 2
        even = old_starts[p] - old_starts[jnp.maximum(p - 1, 0)] - CAP
        return jnp.where(q % 2 == 1, CAP, even)

    nxt = jnp.minimum(b + 1, blocks - 1)
    cut = jnp.clip(tail_end(nxt) - LOW, 0, CAP - LOW)
    low_t = lax.dynamic_slice(table, (0, cut), (D, LOW))
    low_s = lax.dynamic_slice(saved_state, (cut,), (LOW,))
    shift = [(((q - 1) * 2 + rr), q * 2 + rr) for q in range(1, blocks) for rr in range(2)]
    low_t = lax.ppermute(low_t, BOTH, shift)
    low_s = lax.ppermute(low_s, BOTH, shift)
    first = new_starts[b]
    end = jnp.where(b + 1 < blocks, new_starts[nxt], ENTITIES)
    p = jnp.minimum(b // 2, last)
    k = jnp.where(b % 2 == 1, CAP - (first - old_starts[p]), old_starts[p] - first)
    begin = jnp.clip(LOW - k, 0, LOW)
    valid = jnp.arange(CAP, dtype=jnp.int32)[None] < end - first
    own = lax.dynamic_slice(jnp.concatenate([low_t, table], axis=1), (0, begin), (D, CAP))
    own = jnp.where(valid, own, 0.0)
    own_s = lax.dynamic_slice(jnp.concatenate([low_s, saved_state])[None], (0, begin), (1, CAP))
    own_s = jnp.where(valid, own_s, 1.0)

    rows8 = jnp.broadcast_to(own_s, (8, CAP))
    left, state = train_call(blocks, idx[:, 3], idx, own, rows8, relations)
    return left.T, state[0]


def solution(mesh):
    return jax.shard_map(
        functools.partial(local, mesh.shape["blk"]),
        mesh=mesh,
        in_specs=(
            P("blk", None),
            P("blk"),
            P(),
            P(),
            P(),
            P("blk", None, None, None),
            P("blk", None, None, None),
            P("blk", None, None, None),
            P("blk", None, None, None),
            P("blk", None),
        ),
        out_specs=(P(("blk", "rep"), None), P(("blk", "rep"))),
        check_vma=False,
    )
```

```python
import functools

import jax
import jax.numpy as jnp
from jax import lax
from jax.experimental import pallas as pl
from jax.experimental.pallas import tpu as pltpu
from jax.sharding import PartitionSpec as P

LR = 0.2
EPS = 1e-10
F32 = jnp.float32
BF = jnp.bfloat16
D = 400
H = 200
CAP = 1024
HALF = 512
E = 1024
N = 512
CH = 512
LOW = 192
OLD_CAP = 2048
ENTITIES = 122880
STEPS = 4
MESH = pl.DeviceIdType.MESH
ROWS_W = 512
VMEM_LIMIT = 62 * 1024 * 1024
NT = (((1,), (1,)), ((), ()))
NN = (((1,), (0,)), ((), ()))
BOTH = ("blk", "rep")
VMEM = pl.BlockSpec(memory_space=pltpu.VMEM)
ANY = pl.BlockSpec(memory_space=pl.ANY)
SMEM = pl.BlockSpec(memory_space=pltpu.SMEM)


def dot(a, b, dims):
    return lax.dot_general(a, b, dims, preferred_element_type=F32)


def split_to(ref, col, x):
    hi = x.astype(BF)
    ref[0:D, col] = hi
    ref[D : 2 * D, col] = (x - hi.astype(F32)).astype(BF)


def remote(src, dst, send, recv, device):
    return pltpu.make_async_remote_copy(
        src_ref=src, dst_ref=dst, send_sem=send, recv_sem=recv, device_id=device,
        device_id_type=MESH)


def train_kernel(blocks, ids, idx, own, own_state, rel, rel_end, out, out_state,
                 tab, st, rel_s, rel_t, rows, left, state, lhl, rhl, ohs, oht, gshl, gdhl,
                 q_s, g_s, d_s, dp_s, qb_s, dn_s, glo, gli, gro, gri, gsum, carr, lfin, sfin,
                 local_sem, tab_send, tab_recv, gl_send, gl_recv, gr_send, gr_recv,
                 home_send, home_recv, fin_send, fin_recv):
    b = lax.axis_index("blk")
    r = lax.axis_index("rep")
    c = lax.rem(b, 2)
    m2 = b - c
    sibling = (m2 + 1 - c, r)
    ahead = (lax.rem(b + 2, blocks), r)
    behind = (lax.rem(b + blocks - 2, blocks), r)
    ahead_far = (lax.rem(b + 4, blocks), r)
    behind_far = (lax.rem(b + blocks - 4, blocks), r)
    here = c == r
    mine = pl.ds(pl.multiple_of(c * HALF, HALF), HALF)
    theirs = pl.ds(pl.multiple_of((1 - c) * HALF, HALF), HALF)

    def home(s):
        return (lax.rem(m2 + r - s + blocks, blocks), c)

    def origin(s):
        i = lax.rem(b + s, blocks)
        odd = lax.rem(i, 2)
        return (i - odd + r, odd)

    full = rel.shape[1] // CAP

    def get_rel(k):
        if k == full:
            return pltpu.make_async_copy(rel_end, gro.at[0, :, 0:128], local_sem.at[0])
        return pltpu.make_async_copy(
            rel.at[:, k * CAP : (k + 1) * CAP], glo.at[k % 2], local_sem.at[4 + k % 2])

    get_own = pltpu.make_async_copy(own, tab.at[0], local_sem.at[1])
    get_state = pltpu.make_async_copy(own_state, st.at[0], local_sem.at[2])
    get_own.start()
    get_state.start()
    for k in range(min(2, full)):
        get_rel(k).start()
    get_rel(full).start()

    barrier = pltpu.get_barrier_semaphore()
    pl.semaphore_signal(barrier, inc=1, device_id=sibling, device_id_type=MESH)
    pl.semaphore_signal(barrier, inc=1, device_id=behind, device_id_type=MESH)
    for s in range(1, STEPS):
        pl.semaphore_signal(barrier, inc=1, device_id=origin(s), device_id_type=MESH)

    @pl.when(jnp.logical_not(here))
    def _():
        pl.semaphore_signal(barrier, inc=1, device_id=origin(0), device_id_type=MESH)

    @pl.when(r == 0)
    def _():
        pl.semaphore_signal(barrier, inc=1, device_id=behind_far, device_id_type=MESH)

    pl.semaphore_wait(barrier, STEPS + 3 - r - here.astype(jnp.int32))

    share = remote(tab.at[0], tab.at[1], tab_send.at[0], tab_recv.at[0], sibling)
    share_state = remote(st.at[0], st.at[1], tab_send.at[1], tab_recv.at[1], sibling)
    onward = remote(tab.at[0], tab.at[2], tab_send.at[2], tab_recv.at[2], ahead)
    share_on = remote(tab.at[2], tab.at[3], tab_send.at[3], tab_recv.at[3], sibling)
    far = remote(tab.at[1 - c, :, mine], tab.at[4, :, mine], tab_send.at[4], tab_recv.at[4], ahead_far)
    share_far = remote(tab.at[4, :, mine], tab.at[4, :, mine], tab_send.at[5], tab_recv.at[5], sibling)
    share_far_in = remote(tab.at[4, :, theirs], tab.at[4, :, theirs], tab_send.at[5], tab_recv.at[5], sibling)

    def gl_copy(s, k):
        p = lax.rem(s, 2)
        part = theirs if k == 0 else mine
        return remote(glo.at[p, :, part], gli.at[p, :, part], gl_send.at[p, k], gl_recv.at[p, k], sibling)

    def gr_copy(s):
        p = lax.rem(s, 2)
        return remote(gro.at[p], gri.at[p], gr_send.at[p], gr_recv.at[p], sibling)

    def home_copy(s):
        p = lax.rem(s, 2)
        return remote(gsum.at[p], carr.at[s], home_send.at[p], home_recv.at[s], home(s))

    def home_local(s):
        return pltpu.make_async_copy(gsum.at[0], carr.at[0], local_sem.at[3])

    get_own.wait()
    get_state.wait()
    share.start()
    share_state.start()

    @pl.when(c == 1)
    def _():
        onward.start()

    for k in range(full):
        get_rel(k).wait()

        def turn(i, carry):
            at = pl.multiple_of(i * 128, 128)
            rel_s[pl.ds(pl.multiple_of(k * CAP + at, 128), 128), :] = glo[k % 2, :, pl.ds(at, 128)].T
            return carry

        lax.fori_loop(0, CAP // 128, turn, 0)
        if k + 2 < full:
            get_rel(k + 2).start()
    get_rel(full).wait()
    rel_s[full * CAP :, :] = gro[0, :, 0:128].T[0 : rel.shape[1] - full * CAP]

    def gather(s):
        def body(k, carry):
            base = pl.multiple_of(k * 128, 128)
            for i in range(128):
                rows[i : i + 1, 0:D] = rel_s[pl.ds(ids[s, base + i], 1), :]
            rel_t[:, pl.ds(base, 128)] = rows[...].T[0:D]
            return carry

        lax.fori_loop(0, E // 128, body, 0)

    gather(0)
    share.wait_recv()
    share_state.wait_recv()

    @pl.when(r == 0)
    def _():
        far.start()

    state[...] = jnp.where(here, st[0], st[1])
    for c0 in range(0, CAP, 256):
        col = pl.ds(c0, 256)
        x = jnp.where(here, tab[0, :, col], tab[1, :, col])
        left[:, col] = x
        split_to(lhl, col, x)

    def bucket(s, carry):
        p = lax.rem(s, 2)
        same = jnp.where(here, 0, 1)
        slot = jnp.where(
            s == 0, same,
            jnp.where(
                s == 1, jnp.where(r == 0, 3 - c, c),
                jnp.where(s == 2, 2 + same, jnp.where(r == 0, 4, 2 + c))))
        for c0 in range(0, CAP, 256):
            col = pl.ds(c0, 256)
            split_to(rhl, col, tab[slot, :, col])
        row_n = lax.broadcasted_iota(jnp.int32, (CAP, N), 0)
        ohn = jnp.where(row_n == idx[s, 2:3, 0:N], 1.0, 0.0).astype(BF)
        oht[:, E : E + N] = ohn
        nbt = dot(rhl[0:D, :], ohn, NN).astype(BF)
        nb = nbt.T
        for e in range(E // CH):
            col = pl.ds(e * CH, CH)
            live = idx[s, 4:5, col].astype(F32)
            row = lax.broadcasted_iota(jnp.int32, (CAP, CH), 0)
            oh_s = jnp.where(row == idx[s, 0:1, col], 1.0, 0.0).astype(BF)
            ohs[:, col] = oh_s
            sh = dot(lhl[...], oh_s, NN)
            oh_t = jnp.where(row == idx[s, 1:2, col], 1.0, 0.0).astype(BF)
            oht[:, col] = oh_t
            dh = dot(rhl[...], oh_t, NN)
            d = dh[0:D] + dh[D : 2 * D]
            s_re = sh[0:H] + sh[D : D + H]
            s_im = sh[H:D] + sh[D + H : 2 * D]
            r_re = rel_t[0:H, col]
            r_im = rel_t[H:D, col]
            q_s[0:H, :] = s_re * r_re - s_im * r_im
            q_s[H:D, :] = s_re * r_im + s_im * r_re
            q = q_s[...]
            pos = jnp.sum(q * d, axis=0, keepdims=True)
            dpos = -jax.nn.sigmoid(-pos) * live
            d_s[:, col] = d
            dp_s[:, col] = dpos
            split_to(gdhl, col, dpos * q)
            qb = q.astype(BF)
            qb_s[:, col] = qb
            scores = dot(nb, qb, NN)
            dn_s[:, col] = (jax.nn.sigmoid(scores) * (live * (1.0 / N))).astype(BF)
        split_to(gdhl, pl.ds(E, N), dot(qb_s[...], dn_s[...], NT))

        @pl.when(jnp.logical_and(s == 0, c == 0))
        def _():
            onward.start()

        def right_half(part):
            y = dot(gdhl[...], oht[part, :], NT)
            return y[0:D] + y[D : 2 * D]

        def source_grad(e):
            col = pl.ds(e * CH, CH)
            r_re = rel_t[0:H, col]
            r_im = rel_t[H:D, col]
            g_s[...] = dp_s[:, col] * d_s[:, col] + dot(nbt, dn_s[:, col], NN)
            g_re = g_s[0:H, :]
            g_im = g_s[H:D, :]
            q_s[0:H, :] = g_re * r_re + g_im * r_im
            q_s[H:D, :] = g_im * r_re - g_re * r_im
            split_to(gshl, col, q_s[...])

        def left_half(part):
            y = dot(gshl[...], ohs[part, :], NT)
            glo[p, :, part] = y[0:D] + y[D : 2 * D]

        gro[p] = right_half(theirs)
        gr_copy(s).start()
        gsum[p] = right_half(mine)
        source_grad(0)
        gr_copy(s).wait()
        gsum[p] = gsum[p] + gri[p]

        @pl.when(jnp.logical_and(s == 0, here))
        def _():
            home_local(s).start()

        @pl.when(jnp.logical_or(s > 0, jnp.logical_not(here)))
        def _():
            home_copy(s).start()

        for e in range(1, E // CH):
            source_grad(e)
        left_half(theirs)
        gl_copy(s, 0).start()
        left_half(mine)

        @pl.when(s < STEPS - 1)
        def _():
            gl_copy(s, 1).start()
            gather(s + 1)

        @pl.when(s == 0)
        def _():
            @pl.when(c == 0)
            def _():
                share_on.wait_recv()

            @pl.when(c == 1)
            def _():
                onward.wait_recv()
                share_on.start()

        @pl.when(s == 1)
        def _():
            @pl.when(c == 0)
            def _():
                onward.wait_recv()
                share_on.start()

            @pl.when(c == 1)
            def _():
                share_on.wait_recv()

        @pl.when(jnp.logical_and(s == 2, r == 0))
        def _():
            far.wait_recv()
            share_far.start()
            share_far_in.wait_recv()

        @pl.when(jnp.logical_and(s == 1, here))
        def _():
            home_local(s).wait()

        @pl.when(jnp.logical_and(s == 1, jnp.logical_not(here)))
        def _():
            home_copy(0).wait_send()

        @pl.when(s > 1)
        def _():
            home_copy(s - 1).wait_send()

        gl_copy(s, 0).wait_send()
        gl_in = remote(glo.at[p, :, mine], gli.at[p, :, mine], gl_send.at[p, 0], gl_recv.at[p, 0], sibling)
        gl_in.wait_recv()

        @pl.when(s < STEPS - 1)
        def _():
            gl_copy(s, 1).wait_send()
            other = remote(glo.at[p, :, theirs], gli.at[p, :, theirs], gl_send.at[p, 1], gl_recv.at[p, 1], sibling)
            other.wait_recv()
            for c0 in range(0, CAP, 256):
                col = pl.ds(c0, 256)
                g = glo[p, :, col] + gli[p, :, col]
                v = state[:, col] + jnp.sum(g * g, axis=0, keepdims=True) * (1.0 / D)
                x = left[:, col] - LR * g / (jnp.sqrt(v[0:1]) + EPS)
                state[:, col] = v
                left[:, col] = x
                split_to(lhl, col, x)

        return carry

    lax.fori_loop(0, STEPS, bucket, 0)

    p = (STEPS - 1) % 2
    g = glo[p, :, mine] + gli[p, :, mine]
    v = state[:, mine] + jnp.sum(g * g, axis=0, keepdims=True) * (1.0 / D)
    lfin[0] = left[:, mine] - LR * g / (jnp.sqrt(v[0:1]) + EPS)
    sfin[0] = v
    fin = remote(lfin.at[0], lfin.at[1], fin_send.at[0], fin_recv.at[0], home(0))
    fin_state = remote(sfin.at[0], sfin.at[1], fin_send.at[1], fin_recv.at[1], home(0))
    fin_here = pltpu.make_async_copy(lfin.at[0], lfin.at[1], local_sem.at[0])
    fin_state_here = pltpu.make_async_copy(sfin.at[0], sfin.at[1], local_sem.at[1])

    @pl.when(here)
    def _():
        fin_here.start()
        fin_state_here.start()

    @pl.when(jnp.logical_not(here))
    def _():
        fin.start()
        fin_state.start()
        home_copy(0).wait_recv()

    share.wait_send()
    share_state.wait_send()
    onward.wait_send()
    share_on.wait_send()

    @pl.when(r == 0)
    def _():
        far.wait_send()
        share_far.wait_send()

    for s in range(1, STEPS):
        home_copy(s).wait_recv()
    total = (carr[0] + carr[1]) + (carr[2] + carr[3])

    @pl.when(here)
    def _():
        fin_here.wait()
        fin_state_here.wait()

    @pl.when(jnp.logical_not(here))
    def _():
        fin.wait()
        fin_state.wait()

    v = sfin[1] + jnp.sum(total * total, axis=0, keepdims=True) * (1.0 / D)
    out[...] = lfin[1] - LR * total / (jnp.sqrt(v[0:1]) + EPS)
    out_state[...] = v[0:1]
    home_copy(STEPS - 1).wait_send()


def train_call(blocks, ids, idx, own, own_state, rel, rel_end):
    dma = pltpu.SemaphoreType.DMA
    return pl.pallas_call(
        functools.partial(train_kernel, blocks),
        out_shape=(jax.ShapeDtypeStruct((D, HALF), F32), jax.ShapeDtypeStruct((1, HALF), F32)),
        in_specs=[SMEM, VMEM, ANY, ANY, ANY, ANY],
        out_specs=(VMEM, VMEM),
        scratch_shapes=[
            pltpu.VMEM((5, D, CAP), F32),
            pltpu.VMEM((2, 8, CAP), F32),
            pltpu.VMEM(rel.shape[::-1], F32),
            pltpu.VMEM((D, E), F32),
            pltpu.VMEM((128, ROWS_W), F32),
            pltpu.VMEM((D, CAP), F32),
            pltpu.VMEM((8, CAP), F32),
            pltpu.VMEM((2 * D, CAP), BF),
            pltpu.VMEM((2 * D, CAP), BF),
            pltpu.VMEM((CAP, E), BF),
            pltpu.VMEM((CAP, E + N), BF),
            pltpu.VMEM((2 * D, E), BF),
            pltpu.VMEM((2 * D, E + N), BF),
            pltpu.VMEM((D, CH), F32),
            pltpu.VMEM((D, CH), F32),
            pltpu.VMEM((D, E), F32),
            pltpu.VMEM((1, E), F32),
            pltpu.VMEM((D, E), BF),
            pltpu.VMEM((N, E), BF),
            pltpu.VMEM((2, D, CAP), F32),
            pltpu.VMEM((2, D, CAP), F32),
            pltpu.VMEM((2, D, HALF), F32),
            pltpu.VMEM((2, D, HALF), F32),
            pltpu.VMEM((2, D, HALF), F32),
            pltpu.VMEM((STEPS, D, HALF), F32),
            pltpu.VMEM((2, D, HALF), F32),
            pltpu.VMEM((2, 8, HALF), F32),
            dma((6,)),
            dma((6,)),
            dma((6,)),
            dma((2, 2)),
            dma((2, 2)),
            dma((2,)),
            dma((2,)),
            dma((2,)),
            dma((STEPS,)),
            dma((2,)),
            dma((2,)),
        ],
        compiler_params=pltpu.CompilerParams(
            vmem_limit_bytes=VMEM_LIMIT, collective_id=0, has_side_effects=True),
        cost_estimate=pl.CostEstimate(flops=4 * 10**10, bytes_accessed=10**7, transcendentals=0),
        name="train",
    )(ids, idx, own, own_state, rel, rel_end)


def local(blocks, saved_rows, saved_state, old_starts, new_starts, relations,
          source_rows, target_rows, relation_ids, negative_rows, live_groups):
    b = lax.axis_index("blk")
    r = lax.axis_index("rep")
    c = b % 2

    def move(x, route):
        pairs = []
        for m in range(blocks // 2):
            for rr in range(2):
                for cc in range(2):
                    to = route(m, rr, cc)
                    if to is not None:
                        tb, tr = to
                        pairs.append(((2 * m + cc) * 2 + rr, (tb % blocks) * 2 + tr))
        return lax.ppermute(x, BOTH, pairs)

    def sibling(x):
        return move(x, lambda m, rr, cc: (2 * m + 1 - cc, rr))

    def pad(x, fill=-1):
        return jnp.pad(x, ((0, 0), (0, E - x.shape[1])), constant_values=fill)[:, None]

    def pack(g):
        def one(x):
            return pad(lax.dynamic_index_in_dim(x[0], g, 1, keepdims=False))

        rels = pad(lax.dynamic_index_in_dim(relation_ids[0], g, 1, keepdims=False), 0)
        alive = (g < live_groups[0]).astype(jnp.int32)[:, None]
        alive = pad(jnp.broadcast_to(alive, (STEPS, source_rows.shape[3])), 0)
        parts = [one(source_rows), one(target_rows), one(negative_rows), rels, alive]
        return jnp.concatenate(parts + [jnp.zeros((STEPS, 3, E), jnp.int32)], axis=1)

    theirs = sibling(pack(1 - c))
    idx = jnp.where(c == r, pack(c), theirs)

    table = saved_rows.T
    last = old_starts.shape[0] - 1

    def tail_end(q):
        p = q // 2
        even = old_starts[p] - old_starts[jnp.maximum(p - 1, 0)] - CAP
        return jnp.where(q % 2 == 1, CAP, even)

    nxt = jnp.minimum(b + 1, blocks - 1)
    cut = jnp.clip(tail_end(nxt) - LOW, 0, CAP - LOW)
    low_t = lax.dynamic_slice(table, (0, cut), (D, LOW))
    low_s = lax.dynamic_slice(saved_state, (cut,), (LOW,))
    shift = [(((q - 1) * 2 + rr), q * 2 + rr) for q in range(1, blocks) for rr in range(2)]
    low_t = lax.ppermute(low_t, BOTH, shift)
    low_s = lax.ppermute(low_s, BOTH, shift)
    first = new_starts[b]
    end = jnp.where(b + 1 < blocks, new_starts[nxt], ENTITIES)
    p = jnp.minimum(b // 2, last)
    k = jnp.where(b % 2 == 1, CAP - (first - old_starts[p]), old_starts[p] - first)
    begin = jnp.clip(LOW - k, 0, LOW)
    valid = jnp.arange(CAP, dtype=jnp.int32)[None] < end - first
    own = lax.dynamic_slice(jnp.concatenate([low_t, table], axis=1), (0, begin), (D, CAP))
    own = jnp.where(valid, own, 0.0)
    own_s = lax.dynamic_slice(jnp.concatenate([low_s, saved_state])[None], (0, begin), (1, CAP))
    own_s = jnp.where(valid, own_s, 1.0)

    rows8 = jnp.broadcast_to(own_s, (8, CAP))
    rel = relations.T
    end_at = rel.shape[1] // CAP * CAP
    rel_end = jnp.pad(rel[:, end_at:], ((0, 0), (0, end_at + 128 - rel.shape[1])))
    left, state = train_call(blocks, idx[:, 3], idx, own, rows8, rel, rel_end)
    return left.T, state[0]


def solution(mesh):
    return jax.shard_map(
        functools.partial(local, mesh.shape["blk"]),
        mesh=mesh,
        in_specs=(
            P("blk", None),
            P("blk"),
            P(),
            P(),
            P(),
            P("blk", None, None, None),
            P("blk", None, None, None),
            P("blk", None, None, None),
            P("blk", None, None, None),
            P("blk", None),
        ),
        out_specs=(P(("blk", "rep"), None), P(("blk", "rep"))),
        check_vma=False,
    )
```

```python
import functools

import jax
import jax.numpy as jnp
from jax import lax
from jax.experimental import pallas as pl
from jax.experimental.pallas import tpu as pltpu
from jax.sharding import PartitionSpec as P

LR = 0.2
EPS = 1e-10
F32 = jnp.float32
BF = jnp.bfloat16
D = 400
H = 200
CAP = 1024
HALF = 512
E = 1024
N = 512
CH = 512
LOW = 192
OLD_CAP = 2048
ENTITIES = 122880
STEPS = 4
MESH = pl.DeviceIdType.MESH
ROWS_W = 512
VMEM_LIMIT = 62 * 1024 * 1024
NT = (((1,), (1,)), ((), ()))
NN = (((1,), (0,)), ((), ()))
BOTH = ("blk", "rep")
VMEM = pl.BlockSpec(memory_space=pltpu.VMEM)
ANY = pl.BlockSpec(memory_space=pl.ANY)
SMEM = pl.BlockSpec(memory_space=pltpu.SMEM)


def dot(a, b, dims):
    return lax.dot_general(a, b, dims, preferred_element_type=F32)


def split_to(ref, col, x):
    hi = x.astype(BF)
    ref[0:D, col] = hi
    ref[D : 2 * D, col] = (x - hi.astype(F32)).astype(BF)


def remote(src, dst, send, recv, device):
    return pltpu.make_async_remote_copy(
        src_ref=src, dst_ref=dst, send_sem=send, recv_sem=recv, device_id=device,
        device_id_type=MESH)


def train_kernel(blocks, ids, idx, own, own_state, rel, rel_end, out, out_state,
                 tab, st, rel_s, rel_t, rows, left, state, lhl, rhl, ohs, oht, gshl, gdhl,
                 q_s, g_s, d_s, dp_s, qb_s, dn_s, glo, gli, gro, gri, gsum, carr, lfin, sfin,
                 local_sem, tab_send, tab_recv, gl_send, gl_recv, gr_send, gr_recv,
                 home_send, home_recv, fin_send, fin_recv):
    b = lax.axis_index("blk")
    r = lax.axis_index("rep")
    c = lax.rem(b, 2)
    m2 = b - c
    sibling = (m2 + 1 - c, r)
    ahead = (lax.rem(b + 2, blocks), r)
    behind = (lax.rem(b + blocks - 2, blocks), r)
    across = (b, 1 - r)
    here = c == r
    mine = pl.ds(pl.multiple_of(c * HALF, HALF), HALF)
    theirs = pl.ds(pl.multiple_of((1 - c) * HALF, HALF), HALF)

    def home(s):
        return (lax.rem(m2 + r - s + blocks, blocks), c)

    def origin(s):
        i = lax.rem(b + s, blocks)
        odd = lax.rem(i, 2)
        return (i - odd + r, odd)

    full = rel.shape[1] // CAP

    def get_rel(k):
        if k == full:
            return pltpu.make_async_copy(rel_end, gro.at[0, :, 0:128], local_sem.at[0])
        return pltpu.make_async_copy(
            rel.at[:, k * CAP : (k + 1) * CAP], glo.at[k % 2], local_sem.at[4 + k % 2])

    get_own = pltpu.make_async_copy(own, tab.at[0], local_sem.at[1])
    get_state = pltpu.make_async_copy(own_state, st.at[0], local_sem.at[2])
    get_own.start()
    get_state.start()
    for k in range(min(2, full)):
        get_rel(k).start()
    get_rel(full).start()

    barrier = pltpu.get_barrier_semaphore()
    pl.semaphore_signal(barrier, inc=1, device_id=sibling, device_id_type=MESH)
    pl.semaphore_signal(barrier, inc=1, device_id=behind, device_id_type=MESH)
    for s in range(1, STEPS):
        pl.semaphore_signal(barrier, inc=1, device_id=origin(s), device_id_type=MESH)

    @pl.when(jnp.logical_not(here))
    def _():
        pl.semaphore_signal(barrier, inc=1, device_id=origin(0), device_id_type=MESH)

    @pl.when(r + c == 0)
    def _():
        pl.semaphore_signal(barrier, inc=1, device_id=across, device_id_type=MESH)

    pl.semaphore_wait(barrier, STEPS + 2 - here.astype(jnp.int32) + r * (1 - c))

    share = remote(tab.at[0], tab.at[1], tab_send.at[0], tab_recv.at[0], sibling)
    share_state = remote(st.at[0], st.at[1], tab_send.at[1], tab_recv.at[1], sibling)
    onward = remote(tab.at[0], tab.at[2], tab_send.at[2], tab_recv.at[2], ahead)
    relay = remote(tab.at[2], tab.at[2], tab_send.at[6], tab_recv.at[2], across)
    share_on = remote(tab.at[2], tab.at[3], tab_send.at[3], tab_recv.at[3], sibling)
    far = remote(tab.at[3 - c, :, mine], tab.at[4, :, mine], tab_send.at[4], tab_recv.at[4], ahead)
    share_far = remote(tab.at[4, :, mine], tab.at[4, :, mine], tab_send.at[5], tab_recv.at[5], sibling)
    share_far_in = remote(tab.at[4, :, theirs], tab.at[4, :, theirs], tab_send.at[5], tab_recv.at[5], sibling)

    def gl_copy(s, k):
        p = lax.rem(s, 2)
        part = theirs if k == 0 else mine
        return remote(glo.at[p, :, part], gli.at[p, :, part], gl_send.at[p, k], gl_recv.at[p, k], sibling)

    def gr_copy(s):
        p = lax.rem(s, 2)
        return remote(gro.at[p], gri.at[p], gr_send.at[p], gr_recv.at[p], sibling)

    def home_copy(s):
        p = lax.rem(s, 2)
        return remote(gsum.at[p], carr.at[s], home_send.at[p], home_recv.at[s], home(s))

    def home_local(s):
        return pltpu.make_async_copy(gsum.at[0], carr.at[0], local_sem.at[3])

    get_own.wait()
    get_state.wait()
    share.start()
    share_state.start()

    @pl.when(jnp.logical_not(here))
    def _():
        onward.start()

    for k in range(full):
        get_rel(k).wait()

        def turn(i, carry):
            at = pl.multiple_of(i * 128, 128)
            rel_s[pl.ds(pl.multiple_of(k * CAP + at, 128), 128), :] = glo[k % 2, :, pl.ds(at, 128)].T
            return carry

        lax.fori_loop(0, CAP // 128, turn, 0)
        if k + 2 < full:
            get_rel(k + 2).start()
    get_rel(full).wait()
    rel_s[full * CAP :, :] = gro[0, :, 0:128].T[0 : rel.shape[1] - full * CAP]

    def gather(s):
        def body(k, carry):
            base = pl.multiple_of(k * 128, 128)
            for i in range(128):
                rows[i : i + 1, 0:D] = rel_s[pl.ds(ids[s, base + i], 1), :]
            rel_t[:, pl.ds(base, 128)] = rows[...].T[0:D]
            return carry

        lax.fori_loop(0, E // 128, body, 0)

    gather(0)
    share.wait_recv()
    share_state.wait_recv()

    state[...] = jnp.where(here, st[0], st[1])
    for c0 in range(0, CAP, 256):
        col = pl.ds(c0, 256)
        x = jnp.where(here, tab[0, :, col], tab[1, :, col])
        left[:, col] = x
        split_to(lhl, col, x)

    def bucket(s, carry):
        p = lax.rem(s, 2)
        same = jnp.where(here, 0, 1)
        slot = jnp.where(
            s == 0, same,
            jnp.where(
                s == 1, jnp.where(r == 0, 3 - c, c),
                jnp.where(s == 2, 2 + same, jnp.where(r == 0, 4, 2 + c))))
        for c0 in range(0, CAP, 256):
            col = pl.ds(c0, 256)
            split_to(rhl, col, tab[slot, :, col])
        row_n = lax.broadcasted_iota(jnp.int32, (CAP, N), 0)
        ohn = jnp.where(row_n == idx[s, 2:3, 0:N], 1.0, 0.0).astype(BF)
        oht[:, E : E + N] = ohn
        nbt = dot(rhl[0:D, :], ohn, NN).astype(BF)
        nb = nbt.T
        for e in range(E // CH):
            col = pl.ds(e * CH, CH)
            live = idx[s, 4:5, col].astype(F32)
            row = lax.broadcasted_iota(jnp.int32, (CAP, CH), 0)
            oh_s = jnp.where(row == idx[s, 0:1, col], 1.0, 0.0).astype(BF)
            ohs[:, col] = oh_s
            sh = dot(lhl[...], oh_s, NN)
            oh_t = jnp.where(row == idx[s, 1:2, col], 1.0, 0.0).astype(BF)
            oht[:, col] = oh_t
            dh = dot(rhl[...], oh_t, NN)
            d = dh[0:D] + dh[D : 2 * D]
            s_re = sh[0:H] + sh[D : D + H]
            s_im = sh[H:D] + sh[D + H : 2 * D]
            r_re = rel_t[0:H, col]
            r_im = rel_t[H:D, col]
            q_s[0:H, :] = s_re * r_re - s_im * r_im
            q_s[H:D, :] = s_re * r_im + s_im * r_re
            q = q_s[...]
            pos = jnp.sum(q * d, axis=0, keepdims=True)
            dpos = -jax.nn.sigmoid(-pos) * live
            d_s[:, col] = d
            dp_s[:, col] = dpos
            split_to(gdhl, col, dpos * q)
            qb = q.astype(BF)
            qb_s[:, col] = qb
            scores = dot(nb, qb, NN)
            dn_s[:, col] = (jax.nn.sigmoid(scores) * (live * (1.0 / N))).astype(BF)
        split_to(gdhl, pl.ds(E, N), dot(qb_s[...], dn_s[...], NT))

        @pl.when(jnp.logical_and(s == 0, r + c == 2))
        def _():
            onward.start()

        def right_half(part):
            y = dot(gdhl[...], oht[part, :], NT)
            return y[0:D] + y[D : 2 * D]

        def source_grad(e):
            col = pl.ds(e * CH, CH)
            r_re = rel_t[0:H, col]
            r_im = rel_t[H:D, col]
            g_s[...] = dp_s[:, col] * d_s[:, col] + dot(nbt, dn_s[:, col], NN)
            g_re = g_s[0:H, :]
            g_im = g_s[H:D, :]
            q_s[0:H, :] = g_re * r_re + g_im * r_im
            q_s[H:D, :] = g_im * r_re - g_re * r_im
            split_to(gshl, col, q_s[...])

        def left_half(part):
            y = dot(gshl[...], ohs[part, :], NT)
            glo[p, :, part] = y[0:D] + y[D : 2 * D]

        gro[p] = right_half(theirs)
        gr_copy(s).start()
        gsum[p] = right_half(mine)
        source_grad(0)
        gr_copy(s).wait()
        gsum[p] = gsum[p] + gri[p]

        @pl.when(jnp.logical_and(s == 0, here))
        def _():
            home_local(s).start()

        @pl.when(jnp.logical_or(s > 0, jnp.logical_not(here)))
        def _():
            home_copy(s).start()

        for e in range(1, E // CH):
            source_grad(e)
        left_half(theirs)
        gl_copy(s, 0).start()
        left_half(mine)

        @pl.when(s < STEPS - 1)
        def _():
            gl_copy(s, 1).start()
            gather(s + 1)

        @pl.when(jnp.logical_and(s == 0, here) | jnp.logical_and(s == 1, jnp.logical_not(here)))
        def _():
            share_on.wait_recv()

        @pl.when(jnp.logical_and(s == 1, here) | jnp.logical_and(s == 0, jnp.logical_not(here)))
        def _():
            onward.wait_recv()
            share_on.start()

        @pl.when(jnp.logical_and(s == 0, r > c))
        def _():
            relay.start()

        @pl.when(jnp.logical_and(s == 0, r == 0))
        def _():
            far.start()

        @pl.when(jnp.logical_and(s == 2, r == 0))
        def _():
            far.wait_recv()
            share_far.start()
            share_far_in.wait_recv()

        @pl.when(jnp.logical_and(s == 1, here))
        def _():
            home_local(s).wait()

        @pl.when(jnp.logical_and(s == 1, jnp.logical_not(here)))
        def _():
            home_copy(0).wait_send()

        @pl.when(s > 1)
        def _():
            home_copy(s - 1).wait_send()

        gl_copy(s, 0).wait_send()
        gl_in = remote(glo.at[p, :, mine], gli.at[p, :, mine], gl_send.at[p, 0], gl_recv.at[p, 0], sibling)
        gl_in.wait_recv()

        @pl.when(s < STEPS - 1)
        def _():
            gl_copy(s, 1).wait_send()
            other = remote(glo.at[p, :, theirs], gli.at[p, :, theirs], gl_send.at[p, 1], gl_recv.at[p, 1], sibling)
            other.wait_recv()
            for c0 in range(0, CAP, 256):
                col = pl.ds(c0, 256)
                g = glo[p, :, col] + gli[p, :, col]
                v = state[:, col] + jnp.sum(g * g, axis=0, keepdims=True) * (1.0 / D)
                x = left[:, col] - LR * g / (jnp.sqrt(v[0:1]) + EPS)
                state[:, col] = v
                left[:, col] = x
                split_to(lhl, col, x)

        return carry

    lax.fori_loop(0, STEPS, bucket, 0)

    p = (STEPS - 1) % 2
    g = glo[p, :, mine] + gli[p, :, mine]
    v = state[:, mine] + jnp.sum(g * g, axis=0, keepdims=True) * (1.0 / D)
    lfin[0] = left[:, mine] - LR * g / (jnp.sqrt(v[0:1]) + EPS)
    sfin[0] = v
    fin = remote(lfin.at[0], lfin.at[1], fin_send.at[0], fin_recv.at[0], home(0))
    fin_state = remote(sfin.at[0], sfin.at[1], fin_send.at[1], fin_recv.at[1], home(0))
    fin_here = pltpu.make_async_copy(lfin.at[0], lfin.at[1], local_sem.at[0])
    fin_state_here = pltpu.make_async_copy(sfin.at[0], sfin.at[1], local_sem.at[1])

    @pl.when(here)
    def _():
        fin_here.start()
        fin_state_here.start()

    @pl.when(jnp.logical_not(here))
    def _():
        fin.start()
        fin_state.start()
        home_copy(0).wait_recv()

    share.wait_send()
    share_state.wait_send()
    share_on.wait_send()

    @pl.when(r + c > 0)
    def _():
        onward.wait_send()

    @pl.when(r > c)
    def _():
        relay.wait_send()

    @pl.when(r == 0)
    def _():
        far.wait_send()
        share_far.wait_send()

    for s in range(1, STEPS):
        home_copy(s).wait_recv()
    total = (carr[0] + carr[1]) + (carr[2] + carr[3])

    @pl.when(here)
    def _():
        fin_here.wait()
        fin_state_here.wait()

    @pl.when(jnp.logical_not(here))
    def _():
        fin.wait()
        fin_state.wait()

    v = sfin[1] + jnp.sum(total * total, axis=0, keepdims=True) * (1.0 / D)
    out[...] = lfin[1] - LR * total / (jnp.sqrt(v[0:1]) + EPS)
    out_state[...] = v[0:1]
    home_copy(STEPS - 1).wait_send()


def train_call(blocks, ids, idx, own, own_state, rel, rel_end):
    dma = pltpu.SemaphoreType.DMA
    return pl.pallas_call(
        functools.partial(train_kernel, blocks),
        out_shape=(jax.ShapeDtypeStruct((D, HALF), F32), jax.ShapeDtypeStruct((1, HALF), F32)),
        in_specs=[SMEM, VMEM, ANY, ANY, ANY, ANY],
        out_specs=(VMEM, VMEM),
        scratch_shapes=[
            pltpu.VMEM((5, D, CAP), F32),
            pltpu.VMEM((2, 8, CAP), F32),
            pltpu.VMEM(rel.shape[::-1], F32),
            pltpu.VMEM((D, E), F32),
            pltpu.VMEM((128, ROWS_W), F32),
            pltpu.VMEM((D, CAP), F32),
            pltpu.VMEM((8, CAP), F32),
            pltpu.VMEM((2 * D, CAP), BF),
            pltpu.VMEM((2 * D, CAP), BF),
            pltpu.VMEM((CAP, E), BF),
            pltpu.VMEM((CAP, E + N), BF),
            pltpu.VMEM((2 * D, E), BF),
            pltpu.VMEM((2 * D, E + N), BF),
            pltpu.VMEM((D, CH), F32),
            pltpu.VMEM((D, CH), F32),
            pltpu.VMEM((D, E), F32),
            pltpu.VMEM((1, E), F32),
            pltpu.VMEM((D, E), BF),
            pltpu.VMEM((N, E), BF),
            pltpu.VMEM((2, D, CAP), F32),
            pltpu.VMEM((2, D, CAP), F32),
            pltpu.VMEM((2, D, HALF), F32),
            pltpu.VMEM((2, D, HALF), F32),
            pltpu.VMEM((2, D, HALF), F32),
            pltpu.VMEM((STEPS, D, HALF), F32),
            pltpu.VMEM((2, D, HALF), F32),
            pltpu.VMEM((2, 8, HALF), F32),
            dma((6,)),
            dma((7,)),
            dma((6,)),
            dma((2, 2)),
            dma((2, 2)),
            dma((2,)),
            dma((2,)),
            dma((2,)),
            dma((STEPS,)),
            dma((2,)),
            dma((2,)),
        ],
        compiler_params=pltpu.CompilerParams(
            vmem_limit_bytes=VMEM_LIMIT, collective_id=0, has_side_effects=True),
        cost_estimate=pl.CostEstimate(flops=4 * 10**10, bytes_accessed=10**7, transcendentals=0),
        name="train",
    )(ids, idx, own, own_state, rel, rel_end)


def local(blocks, saved_rows, saved_state, old_starts, new_starts, relations,
          source_rows, target_rows, relation_ids, negative_rows, live_groups):
    b = lax.axis_index("blk")
    r = lax.axis_index("rep")
    c = b % 2

    def move(x, route):
        pairs = []
        for m in range(blocks // 2):
            for rr in range(2):
                for cc in range(2):
                    to = route(m, rr, cc)
                    if to is not None:
                        tb, tr = to
                        pairs.append(((2 * m + cc) * 2 + rr, (tb % blocks) * 2 + tr))
        return lax.ppermute(x, BOTH, pairs)

    def sibling(x):
        return move(x, lambda m, rr, cc: (2 * m + 1 - cc, rr))

    def pad(x, fill=-1):
        return jnp.pad(x, ((0, 0), (0, E - x.shape[1])), constant_values=fill)[:, None]

    def pack(g):
        def one(x):
            return pad(lax.dynamic_index_in_dim(x[0], g, 1, keepdims=False))

        rels = pad(lax.dynamic_index_in_dim(relation_ids[0], g, 1, keepdims=False), 0)
        alive = (g < live_groups[0]).astype(jnp.int32)[:, None]
        alive = pad(jnp.broadcast_to(alive, (STEPS, source_rows.shape[3])), 0)
        parts = [one(source_rows), one(target_rows), one(negative_rows), rels, alive]
        return jnp.concatenate(parts + [jnp.zeros((STEPS, 3, E), jnp.int32)], axis=1)

    theirs = sibling(pack(1 - c))
    idx = jnp.where(c == r, pack(c), theirs)

    table = saved_rows.T
    last = old_starts.shape[0] - 1

    def tail_end(q):
        p = q // 2
        even = old_starts[p] - old_starts[jnp.maximum(p - 1, 0)] - CAP
        return jnp.where(q % 2 == 1, CAP, even)

    nxt = jnp.minimum(b + 1, blocks - 1)
    cut = jnp.clip(tail_end(nxt) - LOW, 0, CAP - LOW)
    low_t = lax.dynamic_slice(table, (0, cut), (D, LOW))
    low_s = lax.dynamic_slice(saved_state, (cut,), (LOW,))
    shift = [(((q - 1) * 2 + rr), q * 2 + rr) for q in range(1, blocks) for rr in range(2)]
    low_t = lax.ppermute(low_t, BOTH, shift)
    low_s = lax.ppermute(low_s, BOTH, shift)
    first = new_starts[b]
    end = jnp.where(b + 1 < blocks, new_starts[nxt], ENTITIES)
    p = jnp.minimum(b // 2, last)
    k = jnp.where(b % 2 == 1, CAP - (first - old_starts[p]), old_starts[p] - first)
    begin = jnp.clip(LOW - k, 0, LOW)
    valid = jnp.arange(CAP, dtype=jnp.int32)[None] < end - first
    own = lax.dynamic_slice(jnp.concatenate([low_t, table], axis=1), (0, begin), (D, CAP))
    own = jnp.where(valid, own, 0.0)
    own_s = lax.dynamic_slice(jnp.concatenate([low_s, saved_state])[None], (0, begin), (1, CAP))
    own_s = jnp.where(valid, own_s, 1.0)

    rows8 = jnp.broadcast_to(own_s, (8, CAP))
    rel = relations.T
    end_at = rel.shape[1] // CAP * CAP
    rel_end = jnp.pad(rel[:, end_at:], ((0, 0), (0, end_at + 128 - rel.shape[1])))
    left, state = train_call(blocks, idx[:, 3], idx, own, rows8, rel, rel_end)
    return left.T, state[0]


def solution(mesh):
    return jax.shard_map(
        functools.partial(local, mesh.shape["blk"]),
        mesh=mesh,
        in_specs=(
            P("blk", None),
            P("blk"),
            P(),
            P(),
            P(),
            P("blk", None, None, None),
            P("blk", None, None, None),
            P("blk", None, None, None),
            P("blk", None, None, None),
            P("blk", None),
        ),
        out_specs=(P(("blk", "rep"), None), P(("blk", "rep"))),
        check_vma=False,
    )
```

```python
import functools

import jax
import jax.numpy as jnp
from jax import lax
from jax.experimental import pallas as pl
from jax.experimental.pallas import tpu as pltpu
from jax.sharding import PartitionSpec as P

LR = 0.2
EPS = 1e-10
F32 = jnp.float32
BF = jnp.bfloat16
D = 400
H = 200
CAP = 1024
HALF = 512
E = 1024
N = 512
CH = 512
LOW = 192
OLD_CAP = 2048
ENTITIES = 122880
STEPS = 4
MESH = pl.DeviceIdType.MESH
ROWS_W = 512
VMEM_LIMIT = 62 * 1024 * 1024
NT = (((1,), (1,)), ((), ()))
NN = (((1,), (0,)), ((), ()))
BOTH = ("blk", "rep")
VMEM = pl.BlockSpec(memory_space=pltpu.VMEM)
ANY = pl.BlockSpec(memory_space=pl.ANY)
SMEM = pl.BlockSpec(memory_space=pltpu.SMEM)


def dot(a, b, dims):
    return lax.dot_general(a, b, dims, preferred_element_type=F32)


def split_to(ref, col, x):
    hi = x.astype(BF)
    ref[0:D, col] = hi
    ref[D : 2 * D, col] = (x - hi.astype(F32)).astype(BF)


def remote(src, dst, send, recv, device):
    return pltpu.make_async_remote_copy(
        src_ref=src, dst_ref=dst, send_sem=send, recv_sem=recv, device_id=device,
        device_id_type=MESH)


def train_kernel(blocks, ids, idx, own, own_state, rel, rel_end, out, out_state,
                 tab, st, rel_s, rel_t, rows, left, state, lhl, rhl, ohs, oht, gshl, gdhl,
                 q_s, g_s, d_s, dp_s, qb_s, dn_s, glo, gli, gro, gri, gsum, carr, lfin, sfin,
                 local_sem, tab_send, tab_recv, gl_send, gl_recv, gr_send, gr_recv,
                 home_send, home_recv, fin_send, fin_recv):
    b = lax.axis_index("blk")
    r = lax.axis_index("rep")
    c = lax.rem(b, 2)
    m2 = b - c
    sibling = (m2 + 1 - c, r)
    ahead = (lax.rem(b + 2, blocks), r)
    behind = (lax.rem(b + blocks - 2, blocks), r)
    across = (b, 1 - r)
    here = c == r
    mine = pl.ds(pl.multiple_of(c * HALF, HALF), HALF)
    theirs = pl.ds(pl.multiple_of((1 - c) * HALF, HALF), HALF)

    def home(s):
        return (lax.rem(m2 + r - s + blocks, blocks), c)

    def origin(s):
        i = lax.rem(b + s, blocks)
        odd = lax.rem(i, 2)
        return (i - odd + r, odd)

    full = rel.shape[1] // CAP

    def get_rel(k):
        if k == full:
            return pltpu.make_async_copy(rel_end, gro.at[0, :, 0:128], local_sem.at[0])
        return pltpu.make_async_copy(
            rel.at[:, k * CAP : (k + 1) * CAP], glo.at[k % 2], local_sem.at[4 + k % 2])

    get_own = pltpu.make_async_copy(own, tab.at[0], local_sem.at[1])
    get_state = pltpu.make_async_copy(own_state, st.at[0], local_sem.at[2])
    get_own.start()
    get_state.start()
    for k in range(min(2, full)):
        get_rel(k).start()
    get_rel(full).start()

    barrier = pltpu.get_barrier_semaphore()
    pl.semaphore_signal(barrier, inc=1, device_id=sibling, device_id_type=MESH)
    pl.semaphore_signal(barrier, inc=1, device_id=behind, device_id_type=MESH)
    for s in range(1, STEPS):
        pl.semaphore_signal(barrier, inc=1, device_id=origin(s), device_id_type=MESH)

    @pl.when(jnp.logical_not(here))
    def _():
        pl.semaphore_signal(barrier, inc=1, device_id=origin(0), device_id_type=MESH)

    @pl.when(r + c == 0)
    def _():
        pl.semaphore_signal(barrier, inc=1, device_id=across, device_id_type=MESH)

    pl.semaphore_wait(barrier, STEPS + 2 - here.astype(jnp.int32) + r * (1 - c))

    share = remote(tab.at[0], tab.at[1], tab_send.at[0], tab_recv.at[0], sibling)
    share_state = remote(st.at[0], st.at[1], tab_send.at[1], tab_recv.at[1], sibling)
    t1 = remote(tab.at[0], tab.at[2], tab_send.at[2], tab_recv.at[2], ahead)
    t2a = remote(tab.at[0, :, 0:HALF], tab.at[2, :, 0:HALF], tab_send.at[3], tab_recv.at[3], ahead)
    t2b = remote(tab.at[0, :, HALF:], tab.at[2, :, HALF:], tab_send.at[4], tab_recv.at[4], ahead)
    relay = remote(tab.at[2, :, HALF:], tab.at[2, :, HALF:], tab_send.at[5], tab_recv.at[5], across)
    t3 = remote(tab.at[2], tab.at[4], tab_send.at[6], tab_recv.at[6], ahead)
    share_on = remote(tab.at[2], tab.at[3], tab_send.at[7], tab_recv.at[7], sibling)
    share_far = remote(tab.at[4], tab.at[4], tab_send.at[8], tab_recv.at[8], sibling)

    def gl_copy(s, k):
        p = lax.rem(s, 2)
        part = theirs if k == 0 else mine
        return remote(glo.at[p, :, part], gli.at[p, :, part], gl_send.at[p, k], gl_recv.at[p, k], sibling)

    def gr_copy(s):
        p = lax.rem(s, 2)
        return remote(gro.at[p], gri.at[p], gr_send.at[p], gr_recv.at[p], sibling)

    def home_copy(s):
        p = lax.rem(s, 2)
        return remote(gsum.at[p], carr.at[s], home_send.at[p], home_recv.at[s], home(s))

    def home_local(s):
        return pltpu.make_async_copy(gsum.at[0], carr.at[0], local_sem.at[3])

    get_own.wait()
    get_state.wait()
    share.start()
    share_state.start()

    @pl.when(r < c)
    def _():
        t1.start()

    @pl.when(r > c)
    def _():
        t2b.start()

    for k in range(full):
        get_rel(k).wait()

        def turn(i, carry):
            at = pl.multiple_of(i * 128, 128)
            rel_s[pl.ds(pl.multiple_of(k * CAP + at, 128), 128), :] = glo[k % 2, :, pl.ds(at, 128)].T
            return carry

        lax.fori_loop(0, CAP // 128, turn, 0)
        if k + 2 < full:
            get_rel(k + 2).start()
    get_rel(full).wait()
    rel_s[full * CAP :, :] = gro[0, :, 0:128].T[0 : rel.shape[1] - full * CAP]

    def gather(s):
        def body(k, carry):
            base = pl.multiple_of(k * 128, 128)
            for i in range(128):
                rows[i : i + 1, 0:D] = rel_s[pl.ds(ids[s, base + i], 1), :]
            rel_t[:, pl.ds(base, 128)] = rows[...].T[0:D]
            return carry

        lax.fori_loop(0, E // 128, body, 0)

    gather(0)
    share.wait_recv()
    share_state.wait_recv()

    @pl.when(r + c == 2)
    def _():
        t1.start()


    state[...] = jnp.where(here, st[0], st[1])
    for c0 in range(0, CAP, 256):
        col = pl.ds(c0, 256)
        x = jnp.where(here, tab[0, :, col], tab[1, :, col])
        left[:, col] = x
        split_to(lhl, col, x)

    def bucket(s, carry):
        p = lax.rem(s, 2)
        same = jnp.where(here, 0, 1)
        slot = jnp.where(
            s == 0, same,
            jnp.where(
                s == 1, jnp.where(r == 0, 3 - c, c),
                jnp.where(s == 2, 2 + same, jnp.where(r == 0, 4, 2 + c))))
        for c0 in range(0, CAP, 256):
            col = pl.ds(c0, 256)
            split_to(rhl, col, tab[slot, :, col])
        row_n = lax.broadcasted_iota(jnp.int32, (CAP, N), 0)
        ohn = jnp.where(row_n == idx[s, 2:3, 0:N], 1.0, 0.0).astype(BF)
        oht[:, E : E + N] = ohn
        nbt = dot(rhl[0:D, :], ohn, NN).astype(BF)
        nb = nbt.T
        for e in range(E // CH):
            col = pl.ds(e * CH, CH)
            live = idx[s, 4:5, col].astype(F32)
            row = lax.broadcasted_iota(jnp.int32, (CAP, CH), 0)
            oh_s = jnp.where(row == idx[s, 0:1, col], 1.0, 0.0).astype(BF)
            ohs[:, col] = oh_s
            sh = dot(lhl[...], oh_s, NN)
            oh_t = jnp.where(row == idx[s, 1:2, col], 1.0, 0.0).astype(BF)
            oht[:, col] = oh_t
            dh = dot(rhl[...], oh_t, NN)
            d = dh[0:D] + dh[D : 2 * D]
            s_re = sh[0:H] + sh[D : D + H]
            s_im = sh[H:D] + sh[D + H : 2 * D]
            r_re = rel_t[0:H, col]
            r_im = rel_t[H:D, col]
            q_s[0:H, :] = s_re * r_re - s_im * r_im
            q_s[H:D, :] = s_re * r_im + s_im * r_re
            q = q_s[...]
            pos = jnp.sum(q * d, axis=0, keepdims=True)
            dpos = -jax.nn.sigmoid(-pos) * live
            d_s[:, col] = d
            dp_s[:, col] = dpos
            split_to(gdhl, col, dpos * q)
            qb = q.astype(BF)
            qb_s[:, col] = qb
            scores = dot(nb, qb, NN)
            dn_s[:, col] = (jax.nn.sigmoid(scores) * (live * (1.0 / N))).astype(BF)
        split_to(gdhl, pl.ds(E, N), dot(qb_s[...], dn_s[...], NT))

        @pl.when(jnp.logical_and(s == 0, r + c == 0))
        def _():
            t2a.start()

        @pl.when(jnp.logical_and(s == 0, r > c))
        def _():
            t2b.wait_recv()
            relay.start()

        def right_half(part):
            y = dot(gdhl[...], oht[part, :], NT)
            return y[0:D] + y[D : 2 * D]

        def source_grad(e):
            col = pl.ds(e * CH, CH)
            r_re = rel_t[0:H, col]
            r_im = rel_t[H:D, col]
            g_s[...] = dp_s[:, col] * d_s[:, col] + dot(nbt, dn_s[:, col], NN)
            g_re = g_s[0:H, :]
            g_im = g_s[H:D, :]
            q_s[0:H, :] = g_re * r_re + g_im * r_im
            q_s[H:D, :] = g_im * r_re - g_re * r_im
            split_to(gshl, col, q_s[...])

        def left_half(part):
            y = dot(gshl[...], ohs[part, :], NT)
            glo[p, :, part] = y[0:D] + y[D : 2 * D]

        gro[p] = right_half(theirs)
        gr_copy(s).start()
        gsum[p] = right_half(mine)
        source_grad(0)
        gr_copy(s).wait()
        gsum[p] = gsum[p] + gri[p]

        @pl.when(jnp.logical_and(s == 0, here))
        def _():
            home_local(s).start()

        @pl.when(jnp.logical_or(s > 0, jnp.logical_not(here)))
        def _():
            home_copy(s).start()

        for e in range(1, E // CH):
            source_grad(e)
        left_half(theirs)
        gl_copy(s, 0).start()
        left_half(mine)

        @pl.when(s < STEPS - 1)
        def _():
            gl_copy(s, 1).start()

        @pl.when(jnp.logical_and(s == r, c == 1))
        def _():
            t1.wait_recv()
            share_on.start()

        @pl.when(jnp.logical_and(s == r + 1, c == 0))
        def _():
            t2a.wait_recv()

            @pl.when(r == 0)
            def _():
                relay.wait_recv()

            share_on.start()

        @pl.when(jnp.logical_and(s == 0, r > c))
        def _():
            t2a.start()

        @pl.when(jnp.logical_and(s == 2, r < c))
        def _():
            t3.wait_recv()
            share_far.start()

        @pl.when(s < STEPS - 1)
        def _():
            gather(s + 1)

        @pl.when(jnp.logical_and(s == 0, r < c))
        def _():
            t3.start()

        @pl.when(s == r + c)
        def _():
            share_on.wait_recv()

        @pl.when(jnp.logical_and(s == 2, r + c == 0))
        def _():
            share_far.wait_recv()

        @pl.when(jnp.logical_and(s == 1, here))
        def _():
            home_local(s).wait()

        @pl.when(jnp.logical_and(s == 1, jnp.logical_not(here)))
        def _():
            home_copy(0).wait_send()

        @pl.when(s > 1)
        def _():
            home_copy(s - 1).wait_send()

        gl_copy(s, 0).wait_send()
        gl_in = remote(glo.at[p, :, mine], gli.at[p, :, mine], gl_send.at[p, 0], gl_recv.at[p, 0], sibling)
        gl_in.wait_recv()

        @pl.when(s < STEPS - 1)
        def _():
            gl_copy(s, 1).wait_send()
            other = remote(glo.at[p, :, theirs], gli.at[p, :, theirs], gl_send.at[p, 1], gl_recv.at[p, 1], sibling)
            other.wait_recv()
            for c0 in range(0, CAP, 256):
                col = pl.ds(c0, 256)
                g = glo[p, :, col] + gli[p, :, col]
                v = state[:, col] + jnp.sum(g * g, axis=0, keepdims=True) * (1.0 / D)
                x = left[:, col] - LR * g / (jnp.sqrt(v[0:1]) + EPS)
                state[:, col] = v
                left[:, col] = x
                split_to(lhl, col, x)

        return carry

    lax.fori_loop(0, STEPS, bucket, 0)

    p = (STEPS - 1) % 2
    g = glo[p, :, mine] + gli[p, :, mine]
    v = state[:, mine] + jnp.sum(g * g, axis=0, keepdims=True) * (1.0 / D)
    lfin[0] = left[:, mine] - LR * g / (jnp.sqrt(v[0:1]) + EPS)
    sfin[0] = v
    fin = remote(lfin.at[0], lfin.at[1], fin_send.at[0], fin_recv.at[0], home(0))
    fin_state = remote(sfin.at[0], sfin.at[1], fin_send.at[1], fin_recv.at[1], home(0))
    fin_here = pltpu.make_async_copy(lfin.at[0], lfin.at[1], local_sem.at[0])
    fin_state_here = pltpu.make_async_copy(sfin.at[0], sfin.at[1], local_sem.at[1])

    @pl.when(here)
    def _():
        fin_here.start()
        fin_state_here.start()

    @pl.when(jnp.logical_not(here))
    def _():
        fin.start()
        fin_state.start()
        home_copy(0).wait_recv()

    share.wait_send()
    share_state.wait_send()
    share_on.wait_send()

    @pl.when(c == 1)
    def _():
        t1.wait_send()

    @pl.when(c == 0)
    def _():
        t2a.wait_send()

    @pl.when(r > c)
    def _():
        t2b.wait_send()
        relay.wait_send()

    @pl.when(r < c)
    def _():
        t3.wait_send()
        share_far.wait_send()

    for s in range(1, STEPS):
        home_copy(s).wait_recv()
    total = (carr[0] + carr[1]) + (carr[2] + carr[3])

    @pl.when(here)
    def _():
        fin_here.wait()
        fin_state_here.wait()

    @pl.when(jnp.logical_not(here))
    def _():
        fin.wait()
        fin_state.wait()

    v = sfin[1] + jnp.sum(total * total, axis=0, keepdims=True) * (1.0 / D)
    out[...] = lfin[1] - LR * total / (jnp.sqrt(v[0:1]) + EPS)
    out_state[...] = v[0:1]
    home_copy(STEPS - 1).wait_send()


def train_call(blocks, ids, idx, own, own_state, rel, rel_end):
    dma = pltpu.SemaphoreType.DMA
    return pl.pallas_call(
        functools.partial(train_kernel, blocks),
        out_shape=(jax.ShapeDtypeStruct((D, HALF), F32), jax.ShapeDtypeStruct((1, HALF), F32)),
        in_specs=[SMEM, VMEM, ANY, ANY, ANY, ANY],
        out_specs=(VMEM, VMEM),
        scratch_shapes=[
            pltpu.VMEM((5, D, CAP), F32),
            pltpu.VMEM((2, 8, CAP), F32),
            pltpu.VMEM(rel.shape[::-1], F32),
            pltpu.VMEM((D, E), F32),
            pltpu.VMEM((128, ROWS_W), F32),
            pltpu.VMEM((D, CAP), F32),
            pltpu.VMEM((8, CAP), F32),
            pltpu.VMEM((2 * D, CAP), BF),
            pltpu.VMEM((2 * D, CAP), BF),
            pltpu.VMEM((CAP, E), BF),
            pltpu.VMEM((CAP, E + N), BF),
            pltpu.VMEM((2 * D, E), BF),
            pltpu.VMEM((2 * D, E + N), BF),
            pltpu.VMEM((D, CH), F32),
            pltpu.VMEM((D, CH), F32),
            pltpu.VMEM((D, E), F32),
            pltpu.VMEM((1, E), F32),
            pltpu.VMEM((D, E), BF),
            pltpu.VMEM((N, E), BF),
            pltpu.VMEM((2, D, CAP), F32),
            pltpu.VMEM((2, D, CAP), F32),
            pltpu.VMEM((2, D, HALF), F32),
            pltpu.VMEM((2, D, HALF), F32),
            pltpu.VMEM((2, D, HALF), F32),
            pltpu.VMEM((STEPS, D, HALF), F32),
            pltpu.VMEM((2, D, HALF), F32),
            pltpu.VMEM((2, 8, HALF), F32),
            dma((6,)),
            dma((9,)),
            dma((9,)),
            dma((2, 2)),
            dma((2, 2)),
            dma((2,)),
            dma((2,)),
            dma((2,)),
            dma((STEPS,)),
            dma((2,)),
            dma((2,)),
        ],
        compiler_params=pltpu.CompilerParams(
            vmem_limit_bytes=VMEM_LIMIT, collective_id=0, has_side_effects=True),
        cost_estimate=pl.CostEstimate(flops=4 * 10**10, bytes_accessed=10**7, transcendentals=0),
        name="train",
    )(ids, idx, own, own_state, rel, rel_end)


def local(blocks, saved_rows, saved_state, old_starts, new_starts, relations,
          source_rows, target_rows, relation_ids, negative_rows, live_groups):
    b = lax.axis_index("blk")
    r = lax.axis_index("rep")
    c = b % 2

    def move(x, route):
        pairs = []
        for m in range(blocks // 2):
            for rr in range(2):
                for cc in range(2):
                    to = route(m, rr, cc)
                    if to is not None:
                        tb, tr = to
                        pairs.append(((2 * m + cc) * 2 + rr, (tb % blocks) * 2 + tr))
        return lax.ppermute(x, BOTH, pairs)

    def sibling(x):
        return move(x, lambda m, rr, cc: (2 * m + 1 - cc, rr))

    def pad(x, fill=-1):
        return jnp.pad(x, ((0, 0), (0, E - x.shape[1])), constant_values=fill)[:, None]

    def pack(g):
        def one(x):
            return pad(lax.dynamic_index_in_dim(x[0], g, 1, keepdims=False))

        rels = pad(lax.dynamic_index_in_dim(relation_ids[0], g, 1, keepdims=False), 0)
        alive = (g < live_groups[0]).astype(jnp.int32)[:, None]
        alive = pad(jnp.broadcast_to(alive, (STEPS, source_rows.shape[3])), 0)
        parts = [one(source_rows), one(target_rows), one(negative_rows), rels, alive]
        return jnp.concatenate(parts + [jnp.zeros((STEPS, 3, E), jnp.int32)], axis=1)

    theirs = sibling(pack(1 - c))
    idx = jnp.where(c == r, pack(c), theirs)

    table = saved_rows.T
    last = old_starts.shape[0] - 1

    def tail_end(q):
        p = q // 2
        even = old_starts[p] - old_starts[jnp.maximum(p - 1, 0)] - CAP
        return jnp.where(q % 2 == 1, CAP, even)

    nxt = jnp.minimum(b + 1, blocks - 1)
    cut = jnp.clip(tail_end(nxt) - LOW, 0, CAP - LOW)
    low_t = lax.dynamic_slice(table, (0, cut), (D, LOW))
    low_s = lax.dynamic_slice(saved_state, (cut,), (LOW,))
    shift = [(((q - 1) * 2 + rr), q * 2 + rr) for q in range(1, blocks) for rr in range(2)]
    low_t = lax.ppermute(low_t, BOTH, shift)
    low_s = lax.ppermute(low_s, BOTH, shift)
    first = new_starts[b]
    end = jnp.where(b + 1 < blocks, new_starts[nxt], ENTITIES)
    p = jnp.minimum(b // 2, last)
    k = jnp.where(b % 2 == 1, CAP - (first - old_starts[p]), old_starts[p] - first)
    begin = jnp.clip(LOW - k, 0, LOW)
    valid = jnp.arange(CAP, dtype=jnp.int32)[None] < end - first
    own = lax.dynamic_slice(jnp.concatenate([low_t, table], axis=1), (0, begin), (D, CAP))
    own = jnp.where(valid, own, 0.0)
    own_s = lax.dynamic_slice(jnp.concatenate([low_s, saved_state])[None], (0, begin), (1, CAP))
    own_s = jnp.where(valid, own_s, 1.0)

    rows8 = jnp.broadcast_to(own_s, (8, CAP))
    rel = relations.T
    end_at = rel.shape[1] // CAP * CAP
    rel_end = jnp.pad(rel[:, end_at:], ((0, 0), (0, end_at + 128 - rel.shape[1])))
    left, state = train_call(blocks, idx[:, 3], idx, own, rows8, rel, rel_end)
    return left.T, state[0]


def solution(mesh):
    return jax.shard_map(
        functools.partial(local, mesh.shape["blk"]),
        mesh=mesh,
        in_specs=(
            P("blk", None),
            P("blk"),
            P(),
            P(),
            P(),
            P("blk", None, None, None),
            P("blk", None, None, None),
            P("blk", None, None, None),
            P("blk", None, None, None),
            P("blk", None),
        ),
        out_specs=(P(("blk", "rep"), None), P(("blk", "rep"))),
        check_vma=False,
    )
```

```python
import functools

import jax
import jax.numpy as jnp
from jax import lax
from jax.experimental import pallas as pl
from jax.experimental.pallas import tpu as pltpu
from jax.sharding import PartitionSpec as P

LR = 0.2
EPS = 1e-10
F32 = jnp.float32
BF = jnp.bfloat16
D = 400
H = 200
CAP = 1024
HALF = 512
E = 1024
N = 512
CH = 512
LOW = 256
ENTITIES = 122880
STEPS = 4
MESH = pl.DeviceIdType.MESH
ROWS_W = 512
VMEM_LIMIT = 62 * 1024 * 1024
NT = (((1,), (1,)), ((), ()))
NN = (((1,), (0,)), ((), ()))
BOTH = ("blk", "rep")
VMEM = pl.BlockSpec(memory_space=pltpu.VMEM)
ANY = pl.BlockSpec(memory_space=pl.ANY)
SMEM = pl.BlockSpec(memory_space=pltpu.SMEM)


def dot(a, b, dims):
    return lax.dot_general(a, b, dims, preferred_element_type=F32)


def split_to(ref, col, x):
    hi = x.astype(BF)
    ref[0:D, col] = hi
    ref[D : 2 * D, col] = (x - hi.astype(F32)).astype(BF)


def remote(src, dst, send, recv, device):
    return pltpu.make_async_remote_copy(
        src_ref=src, dst_ref=dst, send_sem=send, recv_sem=recv, device_id=device,
        device_id_type=MESH)


def train_kernel(blocks, ids, old, new, idx, saved, saved_state, rel, rel_end, out, out_state,
                 low_out, low_in, tab, st, rel_s, rel_t, rows, left, state, lhl, rhl, ohs, oht, gshl, gdhl,
                 q_s, g_s, d_s, dp_s, qb_s, dn_s, glo, gli, gro, gri, gsum, carr, lfin, sfin,
                 local_sem, tab_send, tab_recv, gl_send, gl_recv, gr_send, gr_recv,
                 home_send, home_recv, fin_send, fin_recv, low_send, low_recv):
    b = lax.axis_index("blk")
    r = lax.axis_index("rep")
    c = lax.rem(b, 2)
    m2 = b - c
    sibling = (m2 + 1 - c, r)
    ahead = (lax.rem(b + 2, blocks), r)
    behind = (lax.rem(b + blocks - 2, blocks), r)
    across = (b, 1 - r)
    following = (lax.rem(b + 1, blocks), r)
    previous = (lax.rem(b + blocks - 1, blocks), r)
    here = c == r
    mine = pl.ds(pl.multiple_of(c * HALF, HALF), HALF)
    theirs = pl.ds(pl.multiple_of((1 - c) * HALF, HALF), HALF)

    def home(s):
        return (lax.rem(m2 + r - s + blocks, blocks), c)

    def origin(s):
        i = lax.rem(b + s, blocks)
        odd = lax.rem(i, 2)
        return (i - odd + r, odd)

    full = rel.shape[1] // CAP

    def get_rel(k):
        if k == full:
            return pltpu.make_async_copy(rel_end, gro.at[0, :, 0:128], local_sem.at[0])
        return pltpu.make_async_copy(
            rel.at[:, k * CAP : (k + 1) * CAP], glo.at[k % 2], local_sem.at[4 + k % 2])

    get_own = pltpu.make_async_copy(saved, tab.at[0], local_sem.at[1])
    get_own.start()
    for k in range(min(2, full)):
        get_rel(k).start()
    get_rel(full).start()

    low_in[...] = jnp.zeros_like(low_in)
    barrier = pltpu.get_barrier_semaphore()
    pl.semaphore_signal(barrier, inc=1, device_id=sibling, device_id_type=MESH)
    pl.semaphore_signal(barrier, inc=1, device_id=behind, device_id_type=MESH)
    for s in range(1, STEPS):
        pl.semaphore_signal(barrier, inc=1, device_id=origin(s), device_id_type=MESH)

    @pl.when(jnp.logical_not(here))
    def _():
        pl.semaphore_signal(barrier, inc=1, device_id=origin(0), device_id_type=MESH)

    @pl.when(r + c == 0)
    def _():
        pl.semaphore_signal(barrier, inc=1, device_id=across, device_id_type=MESH)

    @pl.when(c == 0)
    def _():
        pl.semaphore_signal(barrier, inc=1, device_id=previous, device_id_type=MESH)

    st[0] = jnp.broadcast_to(saved_state[...], (8, CAP))
    nxt = lax.div(jnp.minimum(b + 1, blocks - 1), 2)
    even_end = old[nxt] - old[jnp.maximum(nxt - 1, 0)] - CAP
    cut = jnp.where(c == 0, CAP, even_end)
    shift = lax.rem(CAP + LOW - cut, CAP)
    get_own.wait()
    for at in range(0, D, 80):
        x = tab[0, at : at + 80, :]
        low_out[at : at + 80, :] = pltpu.roll(x, shift, 1)[:, 0:LOW]
    low_out[D : D + 8, :] = pltpu.roll(st[0], shift, 1)[:, 0:LOW]
    low = remote(low_out, low_in, low_send.at[0], low_recv.at[0], following)
    low_end = remote(low_out.at[:, LOW // 2 :], low_in.at[:, LOW // 2 :], low_send.at[0], low_recv.at[0], following)

    pl.semaphore_wait(barrier, STEPS + 2 - here.astype(jnp.int32) + r * (1 - c) + c)

    @pl.when(c == 0)
    def _():
        low.start()

    @pl.when(c == 1)
    def _():
        low_end.start()

    share = remote(tab.at[0], tab.at[1], tab_send.at[0], tab_recv.at[0], sibling)
    share_state = remote(st.at[0], st.at[1], tab_send.at[1], tab_recv.at[1], sibling)
    t1 = remote(tab.at[0], tab.at[2], tab_send.at[2], tab_recv.at[2], ahead)
    t2a = remote(tab.at[0, :, 0:HALF], tab.at[2, :, 0:HALF], tab_send.at[3], tab_recv.at[3], ahead)
    t2b = remote(tab.at[0, :, HALF:], tab.at[2, :, HALF:], tab_send.at[4], tab_recv.at[4], ahead)
    relay = remote(tab.at[2, :, HALF:], tab.at[2, :, HALF:], tab_send.at[5], tab_recv.at[5], across)
    t3 = remote(tab.at[2], tab.at[4], tab_send.at[6], tab_recv.at[6], ahead)
    share_on = remote(tab.at[2], tab.at[3], tab_send.at[7], tab_recv.at[7], sibling)
    share_far = remote(tab.at[4], tab.at[4], tab_send.at[8], tab_recv.at[8], sibling)

    def gl_copy(s, k):
        p = lax.rem(s, 2)
        part = theirs if k == 0 else mine
        return remote(glo.at[p, :, part], gli.at[p, :, part], gl_send.at[p, k], gl_recv.at[p, k], sibling)

    def gr_copy(s):
        p = lax.rem(s, 2)
        return remote(gro.at[p], gri.at[p], gr_send.at[p], gr_recv.at[p], sibling)

    def home_copy(s):
        p = lax.rem(s, 2)
        return remote(gsum.at[p], carr.at[s], home_send.at[p], home_recv.at[s], home(s))

    def home_local(s):
        return pltpu.make_async_copy(gsum.at[0], carr.at[0], local_sem.at[3])

    def turn_block(k):
        get_rel(k).wait()

        def turn(i, carry):
            at = pl.multiple_of(i * 128, 128)
            rel_s[pl.ds(pl.multiple_of(k * CAP + at, 128), 128), :] = glo[k % 2, :, pl.ds(at, 128)].T
            return carry

        lax.fori_loop(0, CAP // 128, turn, 0)
        if k + 2 < full:
            get_rel(k + 2).start()

    for k in range(min(2, full)):
        turn_block(k)

    @pl.when(c == 1)
    def _():
        low.wait_recv()

    @pl.when(c == 0)
    def _():
        low_end.wait_recv()

    first = new[b]
    start = old[lax.div(b, 2)]
    end = jnp.where(b + 1 < blocks, new[jnp.minimum(b + 1, blocks - 1)], ENTITIES)
    taken = jnp.where(c == 1, CAP - (first - start), start - first)
    lane = lax.broadcasted_iota(jnp.int32, (8, CAP), 1)

    def restored(x, tail, fill):
        y = pltpu.roll(x, taken, 1)
        front = pltpu.roll(tail, taken, 1)
        front = jnp.where(lane[:, 0:LOW] < taken, front, y[:, 0:LOW])
        y = jnp.concatenate([front, y[:, LOW:]], axis=1)
        return jnp.where(lane < end - first, y, fill)

    for at in range(0, D, 8):
        tab[0, at : at + 8, :] = restored(tab[0, at : at + 8, :], low_in[at : at + 8, :], 0.0)
    st[0] = restored(st[0], low_in[D : D + 8, :], 1.0)
    share.start()
    share_state.start()

    @pl.when(r < c)
    def _():
        t1.start()

    @pl.when(r > c)
    def _():
        t2b.start()

    for k in range(min(2, full), full):
        turn_block(k)
    get_rel(full).wait()
    rel_s[full * CAP :, :] = gro[0, :, 0:128].T[0 : rel.shape[1] - full * CAP]

    def gather(s):
        def body(k, carry):
            base = pl.multiple_of(k * 128, 128)
            for i in range(128):
                rows[i : i + 1, 0:D] = rel_s[pl.ds(ids[s, base + i], 1), :]
            rel_t[:, pl.ds(base, 128)] = rows[...].T[0:D]
            return carry

        lax.fori_loop(0, E // 128, body, 0)

    gather(0)
    share.wait_recv()
    share_state.wait_recv()

    @pl.when(r + c == 2)
    def _():
        t1.start()


    state[...] = jnp.where(here, st[0], st[1])
    for c0 in range(0, CAP, 256):
        col = pl.ds(c0, 256)
        x = jnp.where(here, tab[0, :, col], tab[1, :, col])
        left[:, col] = x
        split_to(lhl, col, x)

    def bucket(s, carry):
        p = lax.rem(s, 2)
        same = jnp.where(here, 0, 1)
        slot = jnp.where(
            s == 0, same,
            jnp.where(
                s == 1, jnp.where(r == 0, 3 - c, c),
                jnp.where(s == 2, 2 + same, jnp.where(r == 0, 4, 2 + c))))
        for c0 in range(0, CAP, 256):
            col = pl.ds(c0, 256)
            split_to(rhl, col, tab[slot, :, col])
        row_n = lax.broadcasted_iota(jnp.int32, (CAP, N), 0)
        ohn = jnp.where(row_n == idx[s, 2:3, 0:N], 1.0, 0.0).astype(BF)
        oht[:, E : E + N] = ohn
        nbt = dot(rhl[0:D, :], ohn, NN).astype(BF)
        nb = nbt.T
        for e in range(E // CH):
            col = pl.ds(e * CH, CH)
            live = idx[s, 4:5, col].astype(F32)
            row = lax.broadcasted_iota(jnp.int32, (CAP, CH), 0)
            oh_s = jnp.where(row == idx[s, 0:1, col], 1.0, 0.0).astype(BF)
            ohs[:, col] = oh_s
            sh = dot(lhl[...], oh_s, NN)
            oh_t = jnp.where(row == idx[s, 1:2, col], 1.0, 0.0).astype(BF)
            oht[:, col] = oh_t
            dh = dot(rhl[...], oh_t, NN)
            d = dh[0:D] + dh[D : 2 * D]
            s_re = sh[0:H] + sh[D : D + H]
            s_im = sh[H:D] + sh[D + H : 2 * D]
            r_re = rel_t[0:H, col]
            r_im = rel_t[H:D, col]
            q_s[0:H, :] = s_re * r_re - s_im * r_im
            q_s[H:D, :] = s_re * r_im + s_im * r_re
            q = q_s[...]
            pos = jnp.sum(q * d, axis=0, keepdims=True)
            dpos = -jax.nn.sigmoid(-pos) * live
            d_s[:, col] = d
            dp_s[:, col] = dpos
            split_to(gdhl, col, dpos * q)
            qb = q.astype(BF)
            qb_s[:, col] = qb
            scores = dot(nb, qb, NN)
            dn_s[:, col] = (jax.nn.sigmoid(scores) * (live * (1.0 / N))).astype(BF)
        split_to(gdhl, pl.ds(E, N), dot(qb_s[...], dn_s[...], NT))

        @pl.when(jnp.logical_and(s == 0, r + c == 0))
        def _():
            t2a.start()

        @pl.when(jnp.logical_and(s == 0, r > c))
        def _():
            t2b.wait_recv()
            relay.start()

        def right_half(part):
            y = dot(gdhl[...], oht[part, :], NT)
            return y[0:D] + y[D : 2 * D]

        def source_grad(e):
            col = pl.ds(e * CH, CH)
            r_re = rel_t[0:H, col]
            r_im = rel_t[H:D, col]
            g_s[...] = dp_s[:, col] * d_s[:, col] + dot(nbt, dn_s[:, col], NN)
            g_re = g_s[0:H, :]
            g_im = g_s[H:D, :]
            q_s[0:H, :] = g_re * r_re + g_im * r_im
            q_s[H:D, :] = g_im * r_re - g_re * r_im
            split_to(gshl, col, q_s[...])

        def left_half(part):
            y = dot(gshl[...], ohs[part, :], NT)
            glo[p, :, part] = y[0:D] + y[D : 2 * D]

        gro[p] = right_half(theirs)
        gr_copy(s).start()
        gsum[p] = right_half(mine)
        source_grad(0)
        gr_copy(s).wait()
        gsum[p] = gsum[p] + gri[p]

        @pl.when(jnp.logical_and(s == 0, here))
        def _():
            home_local(s).start()

        @pl.when(jnp.logical_or(s > 0, jnp.logical_not(here)))
        def _():
            home_copy(s).start()

        for e in range(1, E // CH):
            source_grad(e)
        left_half(theirs)
        gl_copy(s, 0).start()
        left_half(mine)

        @pl.when(s < STEPS - 1)
        def _():
            gl_copy(s, 1).start()

        @pl.when(jnp.logical_and(s == r, c == 1))
        def _():
            t1.wait_recv()
            share_on.start()

        @pl.when(jnp.logical_and(s == r + 1, c == 0))
        def _():
            t2a.wait_recv()

            @pl.when(r == 0)
            def _():
                relay.wait_recv()

            share_on.start()

        @pl.when(jnp.logical_and(s == 0, r > c))
        def _():
            t2a.start()

        @pl.when(jnp.logical_and(s == 2, r < c))
        def _():
            t3.wait_recv()
            share_far.start()

        @pl.when(s < STEPS - 1)
        def _():
            gather(s + 1)

        @pl.when(jnp.logical_and(s == 0, r < c))
        def _():
            t3.start()

        @pl.when(s == r + c)
        def _():
            share_on.wait_recv()

        @pl.when(jnp.logical_and(s == 2, r + c == 0))
        def _():
            share_far.wait_recv()

        @pl.when(jnp.logical_and(s == 1, here))
        def _():
            home_local(s).wait()

        @pl.when(jnp.logical_and(s == 1, jnp.logical_not(here)))
        def _():
            home_copy(0).wait_send()

        @pl.when(s > 1)
        def _():
            home_copy(s - 1).wait_send()

        gl_copy(s, 0).wait_send()
        gl_in = remote(glo.at[p, :, mine], gli.at[p, :, mine], gl_send.at[p, 0], gl_recv.at[p, 0], sibling)
        gl_in.wait_recv()

        @pl.when(s < STEPS - 1)
        def _():
            gl_copy(s, 1).wait_send()
            other = remote(glo.at[p, :, theirs], gli.at[p, :, theirs], gl_send.at[p, 1], gl_recv.at[p, 1], sibling)
            other.wait_recv()
            for c0 in range(0, CAP, 256):
                col = pl.ds(c0, 256)
                g = glo[p, :, col] + gli[p, :, col]
                v = state[:, col] + jnp.sum(g * g, axis=0, keepdims=True) * (1.0 / D)
                x = left[:, col] - LR * g / (jnp.sqrt(v[0:1]) + EPS)
                state[:, col] = v
                left[:, col] = x
                split_to(lhl, col, x)

        return carry

    lax.fori_loop(0, STEPS, bucket, 0)

    p = (STEPS - 1) % 2
    g = glo[p, :, mine] + gli[p, :, mine]
    v = state[:, mine] + jnp.sum(g * g, axis=0, keepdims=True) * (1.0 / D)
    lfin[0] = left[:, mine] - LR * g / (jnp.sqrt(v[0:1]) + EPS)
    sfin[0] = v
    fin = remote(lfin.at[0], lfin.at[1], fin_send.at[0], fin_recv.at[0], home(0))
    fin_state = remote(sfin.at[0], sfin.at[1], fin_send.at[1], fin_recv.at[1], home(0))
    fin_here = pltpu.make_async_copy(lfin.at[0], lfin.at[1], local_sem.at[0])
    fin_state_here = pltpu.make_async_copy(sfin.at[0], sfin.at[1], local_sem.at[1])

    @pl.when(here)
    def _():
        fin_here.start()
        fin_state_here.start()

    @pl.when(jnp.logical_not(here))
    def _():
        fin.start()
        fin_state.start()
        home_copy(0).wait_recv()

    share.wait_send()
    share_state.wait_send()
    share_on.wait_send()

    @pl.when(c == 0)
    def _():
        low.wait_send()

    @pl.when(c == 1)
    def _():
        low_end.wait_send()
        t1.wait_send()

    @pl.when(c == 0)
    def _():
        t2a.wait_send()

    @pl.when(r > c)
    def _():
        t2b.wait_send()
        relay.wait_send()

    @pl.when(r < c)
    def _():
        t3.wait_send()
        share_far.wait_send()

    for s in range(1, STEPS):
        home_copy(s).wait_recv()
    total = (carr[0] + carr[1]) + (carr[2] + carr[3])

    @pl.when(here)
    def _():
        fin_here.wait()
        fin_state_here.wait()

    @pl.when(jnp.logical_not(here))
    def _():
        fin.wait()
        fin_state.wait()

    v = sfin[1] + jnp.sum(total * total, axis=0, keepdims=True) * (1.0 / D)
    out[...] = lfin[1] - LR * total / (jnp.sqrt(v[0:1]) + EPS)
    out_state[...] = v[0:1]
    home_copy(STEPS - 1).wait_send()


def train_call(blocks, ids, old, new, idx, saved, saved_state, rel, rel_end):
    dma = pltpu.SemaphoreType.DMA
    return pl.pallas_call(
        functools.partial(train_kernel, blocks),
        out_shape=(jax.ShapeDtypeStruct((D, HALF), F32), jax.ShapeDtypeStruct((1, HALF), F32)),
        in_specs=[SMEM, SMEM, SMEM, VMEM, ANY, VMEM, ANY, ANY],
        out_specs=(VMEM, VMEM),
        scratch_shapes=[
            pltpu.VMEM((D + 8, LOW), F32),
            pltpu.VMEM((D + 8, LOW), F32),
            pltpu.VMEM((5, D, CAP), F32),
            pltpu.VMEM((2, 8, CAP), F32),
            pltpu.VMEM(rel.shape[::-1], F32),
            pltpu.VMEM((D, E), F32),
            pltpu.VMEM((128, ROWS_W), F32),
            pltpu.VMEM((D, CAP), F32),
            pltpu.VMEM((8, CAP), F32),
            pltpu.VMEM((2 * D, CAP), BF),
            pltpu.VMEM((2 * D, CAP), BF),
            pltpu.VMEM((CAP, E), BF),
            pltpu.VMEM((CAP, E + N), BF),
            pltpu.VMEM((2 * D, E), BF),
            pltpu.VMEM((2 * D, E + N), BF),
            pltpu.VMEM((D, CH), F32),
            pltpu.VMEM((D, CH), F32),
            pltpu.VMEM((D, E), F32),
            pltpu.VMEM((1, E), F32),
            pltpu.VMEM((D, E), BF),
            pltpu.VMEM((N, E), BF),
            pltpu.VMEM((2, D, CAP), F32),
            pltpu.VMEM((2, D, CAP), F32),
            pltpu.VMEM((2, D, HALF), F32),
            pltpu.VMEM((2, D, HALF), F32),
            pltpu.VMEM((2, D, HALF), F32),
            pltpu.VMEM((STEPS, D, HALF), F32),
            pltpu.VMEM((2, D, HALF), F32),
            pltpu.VMEM((2, 8, HALF), F32),
            dma((6,)),
            dma((9,)),
            dma((9,)),
            dma((2, 2)),
            dma((2, 2)),
            dma((2,)),
            dma((2,)),
            dma((2,)),
            dma((STEPS,)),
            dma((2,)),
            dma((2,)),
            dma((1,)),
            dma((1,)),
        ],
        compiler_params=pltpu.CompilerParams(
            vmem_limit_bytes=VMEM_LIMIT, collective_id=0, has_side_effects=True),
        cost_estimate=pl.CostEstimate(flops=4 * 10**10, bytes_accessed=10**7, transcendentals=0),
        name="train",
    )(ids, old, new, idx, saved, saved_state, rel, rel_end)


def local(blocks, saved_rows, saved_state, old_starts, new_starts, relations,
          source_rows, target_rows, relation_ids, negative_rows, live_groups):
    b = lax.axis_index("blk")
    r = lax.axis_index("rep")
    c = b % 2

    def move(x, route):
        pairs = []
        for m in range(blocks // 2):
            for rr in range(2):
                for cc in range(2):
                    to = route(m, rr, cc)
                    if to is not None:
                        tb, tr = to
                        pairs.append(((2 * m + cc) * 2 + rr, (tb % blocks) * 2 + tr))
        return lax.ppermute(x, BOTH, pairs)

    def sibling(x):
        return move(x, lambda m, rr, cc: (2 * m + 1 - cc, rr))

    def pad(x, fill=-1):
        return jnp.pad(x, ((0, 0), (0, E - x.shape[1])), constant_values=fill)[:, None]

    def pack(g):
        def one(x):
            return pad(lax.dynamic_index_in_dim(x[0], g, 1, keepdims=False))

        rels = pad(lax.dynamic_index_in_dim(relation_ids[0], g, 1, keepdims=False), 0)
        alive = (g < live_groups[0]).astype(jnp.int32)[:, None]
        alive = pad(jnp.broadcast_to(alive, (STEPS, source_rows.shape[3])), 0)
        parts = [one(source_rows), one(target_rows), one(negative_rows), rels, alive]
        return jnp.concatenate(parts + [jnp.zeros((STEPS, 3, E), jnp.int32)], axis=1)

    theirs = sibling(pack(1 - c))
    idx = jnp.where(c == r, pack(c), theirs)

    rel = relations.T
    end_at = rel.shape[1] // CAP * CAP
    rel_end = jnp.pad(rel[:, end_at:], ((0, 0), (0, end_at + 128 - rel.shape[1])))
    left, state = train_call(
        blocks, idx[:, 3], old_starts, new_starts, idx, saved_rows.T, saved_state[None], rel, rel_end)
    return left.T, state[0]


def solution(mesh):
    return jax.shard_map(
        functools.partial(local, mesh.shape["blk"]),
        mesh=mesh,
        in_specs=(
            P("blk", None),
            P("blk"),
            P(),
            P(),
            P(),
            P("blk", None, None, None),
            P("blk", None, None, None),
            P("blk", None, None, None),
            P("blk", None, None, None),
            P("blk", None),
        ),
        out_specs=(P(("blk", "rep"), None), P(("blk", "rep"))),
        check_vma=False,
    )
```

```python
import functools

import jax
import jax.numpy as jnp
from jax import lax
from jax.experimental import pallas as pl
from jax.experimental.pallas import tpu as pltpu
from jax.sharding import PartitionSpec as P

LR = 0.2
EPS = 1e-10
F32 = jnp.float32
BF = jnp.bfloat16
D = 400
H = 200
CAP = 1024
HALF = 512
E = 1024
N = 512
CH = 512
LOW = 256
ENTITIES = 122880
STEPS = 4
MESH = pl.DeviceIdType.MESH
ROWS_W = 512
VMEM_LIMIT = 62 * 1024 * 1024
NT = (((1,), (1,)), ((), ()))
NN = (((1,), (0,)), ((), ()))
BOTH = ("blk", "rep")
VMEM = pl.BlockSpec(memory_space=pltpu.VMEM)
ANY = pl.BlockSpec(memory_space=pl.ANY)
SMEM = pl.BlockSpec(memory_space=pltpu.SMEM)


def dot(a, b, dims):
    return lax.dot_general(a, b, dims, preferred_element_type=F32)


def split_to(ref, col, x):
    hi = x.astype(BF)
    ref[0:D, col] = hi
    ref[D : 2 * D, col] = (x - hi.astype(F32)).astype(BF)


def remote(src, dst, send, recv, device):
    return pltpu.make_async_remote_copy(
        src_ref=src, dst_ref=dst, send_sem=send, recv_sem=recv, device_id=device,
        device_id_type=MESH)


def train_kernel(blocks, ids, old, new, idx, saved, saved_state, rel, rel_end, out, out_state,
                 low_out, low_in, tab, st, rel_s, rel_t, rows, left, state, lhl, rhl, ohs, oht, gshl, gdhl,
                 q_s, g_s, d_s, dp_s, qb_s, dn_s, glo, gli, gro, gri, gsum, carr, lfin, sfin,
                 local_sem, tab_send, tab_recv, gl_send, gl_recv, gr_send, gr_recv,
                 home_send, home_recv, fin_send, fin_recv, low_send, low_recv):
    b = lax.axis_index("blk")
    r = lax.axis_index("rep")
    c = lax.rem(b, 2)
    m2 = b - c
    sibling = (m2 + 1 - c, r)
    ahead = (lax.rem(b + 2, blocks), r)
    behind = (lax.rem(b + blocks - 2, blocks), r)
    across = (b, 1 - r)
    following = (lax.rem(b + 1, blocks), r)
    previous = (lax.rem(b + blocks - 1, blocks), r)
    here = c == r
    mine = pl.ds(pl.multiple_of(c * HALF, HALF), HALF)
    theirs = pl.ds(pl.multiple_of((1 - c) * HALF, HALF), HALF)

    def home(s):
        return (lax.rem(m2 + r - s + blocks, blocks), c)

    def origin(s):
        i = lax.rem(b + s, blocks)
        odd = lax.rem(i, 2)
        return (i - odd + r, odd)

    full = rel.shape[1] // CAP

    def get_rel(k):
        if k == full:
            return pltpu.make_async_copy(rel_end, gro.at[0, :, 0:128], local_sem.at[0])
        return pltpu.make_async_copy(
            rel.at[:, k * CAP : (k + 1) * CAP], glo.at[k % 2], local_sem.at[4 + k % 2])

    get_own = pltpu.make_async_copy(saved, tab.at[0], local_sem.at[1])
    get_own.start()
    for k in range(min(2, full)):
        get_rel(k).start()
    get_rel(full).start()

    low_in[...] = jnp.zeros_like(low_in)
    barrier = pltpu.get_barrier_semaphore()
    pl.semaphore_signal(barrier, inc=1, device_id=sibling, device_id_type=MESH)
    pl.semaphore_signal(barrier, inc=1, device_id=behind, device_id_type=MESH)
    for s in range(1, STEPS):
        pl.semaphore_signal(barrier, inc=1, device_id=origin(s), device_id_type=MESH)

    @pl.when(jnp.logical_not(here))
    def _():
        pl.semaphore_signal(barrier, inc=1, device_id=origin(0), device_id_type=MESH)

    @pl.when(r + c == 0)
    def _():
        pl.semaphore_signal(barrier, inc=1, device_id=across, device_id_type=MESH)

    @pl.when(c == 0)
    def _():
        pl.semaphore_signal(barrier, inc=1, device_id=previous, device_id_type=MESH)

    st[0] = jnp.broadcast_to(saved_state[...], (8, CAP))
    nxt = lax.div(jnp.minimum(b + 1, blocks - 1), 2)
    even_end = old[nxt] - old[jnp.maximum(nxt - 1, 0)] - CAP
    cut = jnp.where(c == 0, CAP, even_end)
    shift = lax.rem(CAP + LOW - cut, CAP)
    get_own.wait()
    for at in range(0, D, 80):
        x = tab[0, at : at + 80, :]
        low_out[at : at + 80, :] = pltpu.roll(x, shift, 1)[:, 0:LOW]
    low_out[D : D + 8, :] = pltpu.roll(st[0], shift, 1)[:, 0:LOW]
    low = remote(low_out, low_in, low_send.at[0], low_recv.at[0], following)
    low_end = remote(low_out.at[:, LOW // 2 :], low_in.at[:, LOW // 2 :], low_send.at[0], low_recv.at[0], following)

    pl.semaphore_wait(barrier, STEPS + 2 - here.astype(jnp.int32) + r * (1 - c) + c)

    @pl.when(c == 0)
    def _():
        low.start()

    @pl.when(c == 1)
    def _():
        low_end.start()

    share = remote(tab.at[0], tab.at[1], tab_send.at[0], tab_recv.at[0], sibling)
    share_state = remote(st.at[0], st.at[1], tab_send.at[1], tab_recv.at[1], sibling)
    t1 = remote(tab.at[0], tab.at[2], tab_send.at[2], tab_recv.at[2], ahead)
    t2a = remote(tab.at[0, :, 0:HALF], tab.at[2, :, 0:HALF], tab_send.at[3], tab_recv.at[3], ahead)
    t2b = remote(tab.at[0, :, HALF:], tab.at[2, :, HALF:], tab_send.at[4], tab_recv.at[4], ahead)
    relay = remote(tab.at[2, :, HALF:], tab.at[2, :, HALF:], tab_send.at[5], tab_recv.at[5], across)
    t3 = remote(tab.at[2], tab.at[4], tab_send.at[6], tab_recv.at[6], ahead)
    share_on = remote(tab.at[2], tab.at[3], tab_send.at[7], tab_recv.at[7], sibling)
    share_far = remote(tab.at[4], tab.at[4], tab_send.at[8], tab_recv.at[8], sibling)

    def gl_copy(s, k):
        p = lax.rem(s, 2)
        part = theirs if k == 0 else mine
        return remote(glo.at[p, :, part], gli.at[p, :, part], gl_send.at[p, k], gl_recv.at[p, k], sibling)

    def gr_copy(s):
        p = lax.rem(s, 2)
        return remote(gro.at[p], gri.at[p], gr_send.at[p], gr_recv.at[p], sibling)

    def home_copy(s):
        p = lax.rem(s, 2)
        return remote(gsum.at[p], carr.at[s], home_send.at[p], home_recv.at[s], home(s))

    def home_local(s):
        return pltpu.make_async_copy(gsum.at[0], carr.at[0], local_sem.at[3])

    def turn_block(k):
        get_rel(k).wait()

        def turn(i, carry):
            at = pl.multiple_of(i * 128, 128)
            rel_s[pl.ds(pl.multiple_of(k * CAP + at, 128), 128), :] = glo[k % 2, :, pl.ds(at, 128)].T
            return carry

        lax.fori_loop(0, CAP // 128, turn, 0)
        if k + 2 < full:
            get_rel(k + 2).start()

    for k in range(min(2, full)):
        turn_block(k)

    @pl.when(c == 1)
    def _():
        low.wait_recv()

    @pl.when(c == 0)
    def _():
        low_end.wait_recv()

    first = new[b]
    start = old[lax.div(b, 2)]
    end = jnp.where(b + 1 < blocks, new[jnp.minimum(b + 1, blocks - 1)], ENTITIES)
    taken = jnp.where(c == 1, CAP - (first - start), start - first)
    lane = lax.broadcasted_iota(jnp.int32, (8, CAP), 1)

    def restored(x, tail, fill):
        y = pltpu.roll(x, taken, 1)
        front = pltpu.roll(tail, taken, 1)
        front = jnp.where(lane[:, 0:LOW] < taken, front, y[:, 0:LOW])
        y = jnp.concatenate([front, y[:, LOW:]], axis=1)
        return jnp.where(lane < end - first, y, fill)

    for at in range(0, D, 8):
        tab[0, at : at + 8, :] = restored(tab[0, at : at + 8, :], low_in[at : at + 8, :], 0.0)
    st[0] = restored(st[0], low_in[D : D + 8, :], 1.0)
    share.start()
    share_state.start()

    @pl.when(r < c)
    def _():
        t1.start()

    @pl.when(r > c)
    def _():
        t2b.start()

    for k in range(min(2, full), full):
        turn_block(k)
    get_rel(full).wait()
    rel_s[full * CAP :, :] = gro[0, :, 0:128].T[0 : rel.shape[1] - full * CAP]

    def gather_block(s, p, k):
        for i in range(128):
            rows[k % 2, i : i + 1, 0:D] = rel_s[pl.ds(ids[s, k * 128 + i], 1), :]
        rel_t[p, :, k * 128 : (k + 1) * 128] = rows[k % 2].T[0:D]

    for k in range(E // 128):
        gather_block(0, 0, k)
    share.wait_recv()
    share_state.wait_recv()

    @pl.when(r + c == 2)
    def _():
        t1.start()


    state[...] = jnp.where(here, st[0], st[1])
    for c0 in range(0, CAP, 256):
        col = pl.ds(c0, 256)
        x = jnp.where(here, tab[0, :, col], tab[1, :, col])
        left[:, col] = x
        split_to(lhl, col, x)

    def bucket(s, carry):
        p = lax.rem(s, 2)
        same = jnp.where(here, 0, 1)
        slot = jnp.where(
            s == 0, same,
            jnp.where(
                s == 1, jnp.where(r == 0, 3 - c, c),
                jnp.where(s == 2, 2 + same, jnp.where(r == 0, 4, 2 + c))))
        for c0 in range(0, CAP, 256):
            col = pl.ds(c0, 256)
            split_to(rhl, col, tab[slot, :, col])
        row_n = lax.broadcasted_iota(jnp.int32, (CAP, N), 0)
        ohn = jnp.where(row_n == idx[s, 2:3, 0:N], 1.0, 0.0).astype(BF)
        oht[:, E : E + N] = ohn
        nbt = dot(rhl[0:D, :], ohn, NN).astype(BF)
        nb = nbt.T
        for e in range(E // CH):
            col = pl.ds(e * CH, CH)
            live = idx[s, 4:5, col].astype(F32)
            row = lax.broadcasted_iota(jnp.int32, (CAP, CH), 0)
            oh_s = jnp.where(row == idx[s, 0:1, col], 1.0, 0.0).astype(BF)
            ohs[:, col] = oh_s
            sh = dot(lhl[...], oh_s, NN)
            oh_t = jnp.where(row == idx[s, 1:2, col], 1.0, 0.0).astype(BF)
            oht[:, col] = oh_t
            dh = dot(rhl[...], oh_t, NN)
            d = dh[0:D] + dh[D : 2 * D]
            s_re = sh[0:H] + sh[D : D + H]
            s_im = sh[H:D] + sh[D + H : 2 * D]
            r_re = rel_t[p, 0:H, col]
            r_im = rel_t[p, H:D, col]
            q_s[0:H, :] = s_re * r_re - s_im * r_im
            q_s[H:D, :] = s_re * r_im + s_im * r_re
            q = q_s[...]
            pos = jnp.sum(q * d, axis=0, keepdims=True)
            dpos = -jax.nn.sigmoid(-pos) * live
            d_s[:, col] = d
            dp_s[:, col] = dpos
            split_to(gdhl, col, dpos * q)
            qb = q.astype(BF)
            qb_s[:, col] = qb
            scores = dot(nb, qb, NN)
            dn_s[:, col] = (jax.nn.sigmoid(scores) * (live * (1.0 / N))).astype(BF)
            for k in range(CH // 128):
                gather_block(lax.rem(s + 1, STEPS), 1 - p, e * (CH // 128) + k)
        split_to(gdhl, pl.ds(E, N), dot(qb_s[...], dn_s[...], NT))

        @pl.when(jnp.logical_and(s == 0, r + c == 0))
        def _():
            t2a.start()

        @pl.when(jnp.logical_and(s == 0, r > c))
        def _():
            t2b.wait_recv()
            relay.start()

        def right_half(part):
            y = dot(gdhl[...], oht[part, :], NT)
            return y[0:D] + y[D : 2 * D]

        def source_grad(e):
            col = pl.ds(e * CH, CH)
            r_re = rel_t[p, 0:H, col]
            r_im = rel_t[p, H:D, col]
            g_s[...] = dp_s[:, col] * d_s[:, col] + dot(nbt, dn_s[:, col], NN)
            g_re = g_s[0:H, :]
            g_im = g_s[H:D, :]
            q_s[0:H, :] = g_re * r_re + g_im * r_im
            q_s[H:D, :] = g_im * r_re - g_re * r_im
            split_to(gshl, col, q_s[...])

        def left_half(part):
            y = dot(gshl[...], ohs[part, :], NT)
            glo[p, :, part] = y[0:D] + y[D : 2 * D]

        gro[p] = right_half(theirs)
        gr_copy(s).start()
        gsum[p] = right_half(mine)
        source_grad(0)
        gr_copy(s).wait()
        gsum[p] = gsum[p] + gri[p]

        @pl.when(jnp.logical_and(s == 0, here))
        def _():
            home_local(s).start()

        @pl.when(jnp.logical_or(s > 0, jnp.logical_not(here)))
        def _():
            home_copy(s).start()

        @pl.when(jnp.logical_and(s == 1, r + c == 2))
        def _():
            t1.wait_recv()
            share_on.start()

        @pl.when(jnp.logical_and(s == r + 1, c == 0))
        def _():
            t2a.wait_recv()

            @pl.when(r == 0)
            def _():
                relay.wait_recv()

            share_on.start()

        @pl.when(jnp.logical_and(s == 0, r > c))
        def _():
            t2a.start()

        @pl.when(jnp.logical_and(s == 2, r < c))
        def _():
            t3.wait_recv()
            share_far.start()

        for e in range(1, E // CH):
            source_grad(e)
        left_half(theirs)
        gl_copy(s, 0).start()
        left_half(mine)

        @pl.when(s < STEPS - 1)
        def _():
            gl_copy(s, 1).start()

        @pl.when(jnp.logical_and(s == 0, r < c))
        def _():
            t1.wait_recv()
            share_on.start()

        @pl.when(jnp.logical_and(s == 0, r < c))
        def _():
            t3.start()

        @pl.when(jnp.logical_and(s == 1, here))
        def _():
            home_local(s).wait()

        @pl.when(jnp.logical_and(s == 1, jnp.logical_not(here)))
        def _():
            home_copy(0).wait_send()

        @pl.when(s > 1)
        def _():
            home_copy(s - 1).wait_send()

        gl_copy(s, 0).wait_send()
        gl_in = remote(glo.at[p, :, mine], gli.at[p, :, mine], gl_send.at[p, 0], gl_recv.at[p, 0], sibling)
        gl_in.wait_recv()

        @pl.when(s < STEPS - 1)
        def _():
            gl_copy(s, 1).wait_send()
            other = remote(glo.at[p, :, theirs], gli.at[p, :, theirs], gl_send.at[p, 1], gl_recv.at[p, 1], sibling)
            other.wait_recv()
            for c0 in range(0, CAP, 256):
                col = pl.ds(c0, 256)
                g = glo[p, :, col] + gli[p, :, col]
                v = state[:, col] + jnp.sum(g * g, axis=0, keepdims=True) * (1.0 / D)
                x = left[:, col] - LR * g / (jnp.sqrt(v[0:1]) + EPS)
                state[:, col] = v
                left[:, col] = x
                split_to(lhl, col, x)

        @pl.when(s == r + c)
        def _():
            share_on.wait_recv()

        @pl.when(jnp.logical_and(s == 2, r + c == 0))
        def _():
            share_far.wait_recv()

        return carry

    lax.fori_loop(0, STEPS, bucket, 0)

    p = (STEPS - 1) % 2
    g = glo[p, :, mine] + gli[p, :, mine]
    v = state[:, mine] + jnp.sum(g * g, axis=0, keepdims=True) * (1.0 / D)
    lfin[0] = left[:, mine] - LR * g / (jnp.sqrt(v[0:1]) + EPS)
    sfin[0] = v
    fin = remote(lfin.at[0], lfin.at[1], fin_send.at[0], fin_recv.at[0], home(0))
    fin_state = remote(sfin.at[0], sfin.at[1], fin_send.at[1], fin_recv.at[1], home(0))
    fin_here = pltpu.make_async_copy(lfin.at[0], lfin.at[1], local_sem.at[0])
    fin_state_here = pltpu.make_async_copy(sfin.at[0], sfin.at[1], local_sem.at[1])

    @pl.when(here)
    def _():
        fin_here.start()
        fin_state_here.start()

    @pl.when(jnp.logical_not(here))
    def _():
        fin.start()
        fin_state.start()
        home_copy(0).wait_recv()

    share.wait_send()
    share_state.wait_send()
    share_on.wait_send()

    @pl.when(c == 0)
    def _():
        low.wait_send()

    @pl.when(c == 1)
    def _():
        low_end.wait_send()
        t1.wait_send()

    @pl.when(c == 0)
    def _():
        t2a.wait_send()

    @pl.when(r > c)
    def _():
        t2b.wait_send()
        relay.wait_send()

    @pl.when(r < c)
    def _():
        t3.wait_send()
        share_far.wait_send()

    for s in range(1, STEPS):
        home_copy(s).wait_recv()
    total = (carr[0] + carr[1]) + (carr[2] + carr[3])

    @pl.when(here)
    def _():
        fin_here.wait()
        fin_state_here.wait()

    @pl.when(jnp.logical_not(here))
    def _():
        fin.wait()
        fin_state.wait()

    v = sfin[1] + jnp.sum(total * total, axis=0, keepdims=True) * (1.0 / D)
    out[...] = lfin[1] - LR * total / (jnp.sqrt(v[0:1]) + EPS)
    out_state[...] = v[0:1]
    home_copy(STEPS - 1).wait_send()


def train_call(blocks, ids, old, new, idx, saved, saved_state, rel, rel_end):
    dma = pltpu.SemaphoreType.DMA
    return pl.pallas_call(
        functools.partial(train_kernel, blocks),
        out_shape=(jax.ShapeDtypeStruct((D, HALF), F32), jax.ShapeDtypeStruct((1, HALF), F32)),
        in_specs=[SMEM, SMEM, SMEM, VMEM, ANY, VMEM, ANY, ANY],
        out_specs=(VMEM, VMEM),
        scratch_shapes=[
            pltpu.VMEM((D + 8, LOW), F32),
            pltpu.VMEM((D + 8, LOW), F32),
            pltpu.VMEM((5, D, CAP), F32),
            pltpu.VMEM((2, 8, CAP), F32),
            pltpu.VMEM(rel.shape[::-1], F32),
            pltpu.VMEM((2, D, E), F32),
            pltpu.VMEM((2, 128, ROWS_W), F32),
            pltpu.VMEM((D, CAP), F32),
            pltpu.VMEM((8, CAP), F32),
            pltpu.VMEM((2 * D, CAP), BF),
            pltpu.VMEM((2 * D, CAP), BF),
            pltpu.VMEM((CAP, E), BF),
            pltpu.VMEM((CAP, E + N), BF),
            pltpu.VMEM((2 * D, E), BF),
            pltpu.VMEM((2 * D, E + N), BF),
            pltpu.VMEM((D, CH), F32),
            pltpu.VMEM((D, CH), F32),
            pltpu.VMEM((D, E), F32),
            pltpu.VMEM((1, E), F32),
            pltpu.VMEM((D, E), BF),
            pltpu.VMEM((N, E), BF),
            pltpu.VMEM((2, D, CAP), F32),
            pltpu.VMEM((2, D, CAP), F32),
            pltpu.VMEM((2, D, HALF), F32),
            pltpu.VMEM((2, D, HALF), F32),
            pltpu.VMEM((2, D, HALF), F32),
            pltpu.VMEM((STEPS, D, HALF), F32),
            pltpu.VMEM((2, D, HALF), F32),
            pltpu.VMEM((2, 8, HALF), F32),
            dma((6,)),
            dma((9,)),
            dma((9,)),
            dma((2, 2)),
            dma((2, 2)),
            dma((2,)),
            dma((2,)),
            dma((2,)),
            dma((STEPS,)),
            dma((2,)),
            dma((2,)),
            dma((1,)),
            dma((1,)),
        ],
        compiler_params=pltpu.CompilerParams(
            vmem_limit_bytes=VMEM_LIMIT, collective_id=0, has_side_effects=True),
        cost_estimate=pl.CostEstimate(flops=4 * 10**10, bytes_accessed=10**7, transcendentals=0),
        name="train",
    )(ids, old, new, idx, saved, saved_state, rel, rel_end)


def local(blocks, saved_rows, saved_state, old_starts, new_starts, relations,
          source_rows, target_rows, relation_ids, negative_rows, live_groups):
    b = lax.axis_index("blk")
    r = lax.axis_index("rep")
    c = b % 2

    def move(x, route):
        pairs = []
        for m in range(blocks // 2):
            for rr in range(2):
                for cc in range(2):
                    to = route(m, rr, cc)
                    if to is not None:
                        tb, tr = to
                        pairs.append(((2 * m + cc) * 2 + rr, (tb % blocks) * 2 + tr))
        return lax.ppermute(x, BOTH, pairs)

    def sibling(x):
        return move(x, lambda m, rr, cc: (2 * m + 1 - cc, rr))

    def pad(x, fill=-1):
        return jnp.pad(x, ((0, 0), (0, E - x.shape[1])), constant_values=fill)[:, None]

    def pack(g):
        def one(x):
            return pad(lax.dynamic_index_in_dim(x[0], g, 1, keepdims=False))

        rels = pad(lax.dynamic_index_in_dim(relation_ids[0], g, 1, keepdims=False), 0)
        alive = (g < live_groups[0]).astype(jnp.int32)[:, None]
        alive = pad(jnp.broadcast_to(alive, (STEPS, source_rows.shape[3])), 0)
        parts = [one(source_rows), one(target_rows), one(negative_rows), rels, alive]
        return jnp.concatenate(parts + [jnp.zeros((STEPS, 3, E), jnp.int32)], axis=1)

    theirs = sibling(pack(1 - c))
    idx = jnp.where(c == r, pack(c), theirs)

    rel = relations.T
    end_at = rel.shape[1] // CAP * CAP
    rel_end = jnp.pad(rel[:, end_at:], ((0, 0), (0, end_at + 128 - rel.shape[1])))
    left, state = train_call(
        blocks, idx[:, 3], old_starts, new_starts, idx, saved_rows.T, saved_state[None], rel, rel_end)
    return left.T, state[0]


def solution(mesh):
    return jax.shard_map(
        functools.partial(local, mesh.shape["blk"]),
        mesh=mesh,
        in_specs=(
            P("blk", None),
            P("blk"),
            P(),
            P(),
            P(),
            P("blk", None, None, None),
            P("blk", None, None, None),
            P("blk", None, None, None),
            P("blk", None, None, None),
            P("blk", None),
        ),
        out_specs=(P(("blk", "rep"), None), P(("blk", "rep"))),
        check_vma=False,
    )
```

```python
import functools

import jax
import jax.numpy as jnp
from jax import lax
from jax.experimental import pallas as pl
from jax.experimental.pallas import tpu as pltpu
from jax.sharding import PartitionSpec as P

LR = 0.2
EPS = 1e-10
F32 = jnp.float32
BF = jnp.bfloat16
D = 400
H = 200
CAP = 1024
HALF = 512
E = 1024
N = 512
CH = 512
LOW = 256
ENTITIES = 122880
STEPS = 4
MESH = pl.DeviceIdType.MESH
ROWS_W = 512
VMEM_LIMIT = 62 * 1024 * 1024
NT = (((1,), (1,)), ((), ()))
NN = (((1,), (0,)), ((), ()))
BOTH = ("blk", "rep")
VMEM = pl.BlockSpec(memory_space=pltpu.VMEM)
ANY = pl.BlockSpec(memory_space=pl.ANY)
SMEM = pl.BlockSpec(memory_space=pltpu.SMEM)


def dot(a, b, dims):
    return lax.dot_general(a, b, dims, preferred_element_type=F32)


def split_to(ref, col, x):
    hi = x.astype(BF)
    ref[0:D, col] = hi
    ref[D : 2 * D, col] = (x - hi.astype(F32)).astype(BF)


def remote(src, dst, send, recv, device):
    return pltpu.make_async_remote_copy(
        src_ref=src, dst_ref=dst, send_sem=send, recv_sem=recv, device_id=device,
        device_id_type=MESH)


def train_kernel(blocks, ids, old, new, idx, saved, saved_state, rel, rel_end, out, out_state,
                 low_out, low_in, tab, st, rel_s, rel_t, rows, left, state, lhl, rhl, ohs, oht, gshl, gdhl,
                 q_s, g_s, d_s, dp_s, qb_s, dn_s, glo, gli, gro, gri, gsum, carr, lfin, sfin,
                 local_sem, tab_send, tab_recv, gl_send, gl_recv, gr_send, gr_recv,
                 home_send, home_recv, fin_send, fin_recv, low_send, low_recv):
    b = lax.axis_index("blk")
    r = lax.axis_index("rep")
    c = lax.rem(b, 2)
    m2 = b - c
    sibling = (m2 + 1 - c, r)
    ahead = (lax.rem(b + 2, blocks), r)
    behind = (lax.rem(b + blocks - 2, blocks), r)
    across = (b, 1 - r)
    following = (lax.rem(b + 1, blocks), r)
    previous = (lax.rem(b + blocks - 1, blocks), r)
    here = c == r
    mine = pl.ds(pl.multiple_of(c * HALF, HALF), HALF)
    theirs = pl.ds(pl.multiple_of((1 - c) * HALF, HALF), HALF)

    def home(s):
        return (lax.rem(m2 + r - s + blocks, blocks), c)

    def origin(s):
        i = lax.rem(b + s, blocks)
        odd = lax.rem(i, 2)
        return (i - odd + r, odd)

    full = rel.shape[1] // CAP

    def get_rel(k):
        if k == full:
            return pltpu.make_async_copy(rel_end, gro.at[0, :, 0:128], local_sem.at[0])
        return pltpu.make_async_copy(
            rel.at[:, k * CAP : (k + 1) * CAP], glo.at[k % 2], local_sem.at[4 + k % 2])

    get_own = pltpu.make_async_copy(saved, tab.at[0], local_sem.at[1])
    get_own.start()
    for k in range(min(2, full)):
        get_rel(k).start()
    get_rel(full).start()

    low_in[...] = jnp.zeros_like(low_in)
    barrier = pltpu.get_barrier_semaphore()
    pl.semaphore_signal(barrier, inc=1, device_id=sibling, device_id_type=MESH)
    pl.semaphore_signal(barrier, inc=1, device_id=behind, device_id_type=MESH)
    for s in range(1, STEPS):
        pl.semaphore_signal(barrier, inc=1, device_id=origin(s), device_id_type=MESH)

    @pl.when(jnp.logical_not(here))
    def _():
        pl.semaphore_signal(barrier, inc=1, device_id=origin(0), device_id_type=MESH)

    @pl.when(r + c == 0)
    def _():
        pl.semaphore_signal(barrier, inc=1, device_id=across, device_id_type=MESH)

    @pl.when(c == 0)
    def _():
        pl.semaphore_signal(barrier, inc=1, device_id=previous, device_id_type=MESH)

    st[0] = jnp.broadcast_to(saved_state[...], (8, CAP))
    nxt = lax.div(jnp.minimum(b + 1, blocks - 1), 2)
    even_end = old[nxt] - old[jnp.maximum(nxt - 1, 0)] - CAP
    cut = jnp.where(c == 0, CAP, even_end)
    shift = lax.rem(CAP + LOW - cut, CAP)
    get_own.wait()
    for at in range(0, D, 80):
        x = tab[0, at : at + 80, :]
        low_out[at : at + 80, :] = pltpu.roll(x, shift, 1)[:, 0:LOW]
    low_out[D : D + 8, :] = pltpu.roll(st[0], shift, 1)[:, 0:LOW]
    low = remote(low_out, low_in, low_send.at[0], low_recv.at[0], following)
    low_end = remote(low_out.at[:, LOW // 2 :], low_in.at[:, LOW // 2 :], low_send.at[0], low_recv.at[0], following)

    pl.semaphore_wait(barrier, STEPS + 2 - here.astype(jnp.int32) + r * (1 - c) + c)

    @pl.when(c == 0)
    def _():
        low.start()

    @pl.when(c == 1)
    def _():
        low_end.start()

    share = remote(tab.at[0], tab.at[1], tab_send.at[0], tab_recv.at[0], sibling)
    share_state = remote(st.at[0], st.at[1], tab_send.at[1], tab_recv.at[1], sibling)
    t1 = remote(tab.at[0], tab.at[2], tab_send.at[2], tab_recv.at[2], ahead)
    t2a = remote(tab.at[0, :, 0:HALF], tab.at[2, :, 0:HALF], tab_send.at[3], tab_recv.at[3], ahead)
    t2b = remote(tab.at[0, :, HALF:], tab.at[2, :, HALF:], tab_send.at[4], tab_recv.at[4], ahead)
    relay = remote(tab.at[2, :, HALF:], tab.at[2, :, HALF:], tab_send.at[5], tab_recv.at[5], across)
    t3 = remote(tab.at[2], tab.at[4], tab_send.at[6], tab_recv.at[6], ahead)
    share_on = remote(tab.at[2], tab.at[3], tab_send.at[7], tab_recv.at[7], sibling)
    share_far = remote(tab.at[4], tab.at[4], tab_send.at[8], tab_recv.at[8], sibling)

    def gl_copy(s, k):
        p = lax.rem(s, 2)
        part = theirs if k == 0 else mine
        return remote(glo.at[p, :, part], gli.at[p, :, part], gl_send.at[p, k], gl_recv.at[p, k], sibling)

    def gr_copy(s):
        p = lax.rem(s, 2)
        return remote(gro.at[p], gri.at[p], gr_send.at[p], gr_recv.at[p], sibling)

    def home_copy(s):
        p = lax.rem(s, 2)
        return remote(gsum.at[p], carr.at[s], home_send.at[p], home_recv.at[s], home(s))

    def home_local(s):
        return pltpu.make_async_copy(gsum.at[0], carr.at[0], local_sem.at[3])

    def turn_block(k):
        get_rel(k).wait()

        def turn(i, carry):
            at = pl.multiple_of(i * 128, 128)
            rel_s[pl.ds(pl.multiple_of(k * CAP + at, 128), 128), :] = glo[k % 2, :, pl.ds(at, 128)].T
            return carry

        lax.fori_loop(0, CAP // 128, turn, 0)
        if k + 2 < full:
            get_rel(k + 2).start()

    for k in range(min(2, full)):
        turn_block(k)

    @pl.when(c == 1)
    def _():
        low.wait_recv()

    @pl.when(c == 0)
    def _():
        low_end.wait_recv()

    first = new[b]
    start = old[lax.div(b, 2)]
    end = jnp.where(b + 1 < blocks, new[jnp.minimum(b + 1, blocks - 1)], ENTITIES)
    taken = jnp.where(c == 1, CAP - (first - start), start - first)
    lane = lax.broadcasted_iota(jnp.int32, (8, CAP), 1)

    def restored(x, tail, fill):
        y = pltpu.roll(x, taken, 1)
        front = pltpu.roll(tail, taken, 1)
        front = jnp.where(lane[:, 0:LOW] < taken, front, y[:, 0:LOW])
        y = jnp.concatenate([front, y[:, LOW:]], axis=1)
        return jnp.where(lane < end - first, y, fill)

    for at in range(0, D, 8):
        tab[0, at : at + 8, :] = restored(tab[0, at : at + 8, :], low_in[at : at + 8, :], 0.0)
    st[0] = restored(st[0], low_in[D : D + 8, :], 1.0)
    share.start()
    share_state.start()

    @pl.when(r < c)
    def _():
        t1.start()

    @pl.when(r > c)
    def _():
        t2b.start()

    for k in range(min(2, full), full):
        turn_block(k)
    get_rel(full).wait()
    rel_s[full * CAP :, :] = gro[0, :, 0:128].T[0 : rel.shape[1] - full * CAP]

    def gather_block(s, p, k):
        for i in range(128):
            rows[k % 2, i : i + 1, 0:D] = rel_s[pl.ds(ids[s, k * 128 + i], 1), :]
        rel_t[p, :, k * 128 : (k + 1) * 128] = rows[k % 2].T[0:D]

    for k in range(E // 128):
        gather_block(0, 0, k)
    share.wait_recv()
    share_state.wait_recv()

    @pl.when(r + c == 2)
    def _():
        t1.start()


    state[...] = jnp.where(here, st[0], st[1])
    for c0 in range(0, CAP, 256):
        col = pl.ds(c0, 256)
        x = jnp.where(here, tab[0, :, col], tab[1, :, col])
        left[:, col] = x
        split_to(lhl, col, x)

    def bucket(s, carry):
        p = lax.rem(s, 2)
        same = jnp.where(here, 0, 1)
        slot = jnp.where(
            s == 0, same,
            jnp.where(
                s == 1, jnp.where(r == 0, 3 - c, c),
                jnp.where(s == 2, 2 + same, jnp.where(r == 0, 4, 2 + c))))
        for c0 in range(0, CAP, 256):
            col = pl.ds(c0, 256)
            split_to(rhl, col, tab[slot, :, col])
        row_n = lax.broadcasted_iota(jnp.int32, (CAP, N), 0)
        ohn = jnp.where(row_n == idx[s, 2:3, 0:N], 1.0, 0.0).astype(BF)
        oht[:, E : E + N] = ohn
        nbt = dot(rhl[0:D, :], ohn, NN).astype(BF)
        nb = nbt.T
        for e in range(E // CH):
            col = pl.ds(e * CH, CH)
            live = idx[s, 4:5, col].astype(F32)
            row = lax.broadcasted_iota(jnp.int32, (CAP, CH), 0)
            oh_s = jnp.where(row == idx[s, 0:1, col], 1.0, 0.0).astype(BF)
            ohs[:, col] = oh_s
            sh = dot(lhl[...], oh_s, NN)
            oh_t = jnp.where(row == idx[s, 1:2, col], 1.0, 0.0).astype(BF)
            oht[:, col] = oh_t
            dh = dot(rhl[...], oh_t, NN)
            d = dh[0:D] + dh[D : 2 * D]
            s_re = sh[0:H] + sh[D : D + H]
            s_im = sh[H:D] + sh[D + H : 2 * D]
            r_re = rel_t[p, 0:H, col]
            r_im = rel_t[p, H:D, col]
            q_s[0:H, :] = s_re * r_re - s_im * r_im
            q_s[H:D, :] = s_re * r_im + s_im * r_re
            q = q_s[...]
            pos = jnp.sum(q * d, axis=0, keepdims=True)
            dpos = -jax.nn.sigmoid(-pos) * live
            d_s[:, col] = d
            dp_s[:, col] = dpos
            split_to(gdhl, col, dpos * q)
            qb = q.astype(BF)
            qb_s[:, col] = qb
            scores = dot(nb, qb, NN)
            dn_s[:, col] = (jax.nn.sigmoid(scores) * (live * (1.0 / N))).astype(BF)
            for k in range(CH // 128):
                gather_block(lax.rem(s + 1, STEPS), 1 - p, e * (CH // 128) + k)
        split_to(gdhl, pl.ds(E, N), dot(qb_s[...], dn_s[...], NT))

        @pl.when(jnp.logical_and(s == 0, r > c))
        def _():
            t2b.wait_recv()
            relay.start()

        def right_half(part):
            y = dot(gdhl[...], oht[part, :], NT)
            return y[0:D] + y[D : 2 * D]

        def source_grad(e):
            col = pl.ds(e * CH, CH)
            r_re = rel_t[p, 0:H, col]
            r_im = rel_t[p, H:D, col]
            g_s[...] = dp_s[:, col] * d_s[:, col] + dot(nbt, dn_s[:, col], NN)
            g_re = g_s[0:H, :]
            g_im = g_s[H:D, :]
            q_s[0:H, :] = g_re * r_re + g_im * r_im
            q_s[H:D, :] = g_im * r_re - g_re * r_im
            split_to(gshl, col, q_s[...])

        def left_half(part):
            y = dot(gshl[...], ohs[part, :], NT)
            glo[p, :, part] = y[0:D] + y[D : 2 * D]

        gro[p] = right_half(theirs)
        gr_copy(s).start()
        gsum[p] = right_half(mine)
        source_grad(0)
        gr_copy(s).wait()
        gsum[p] = gsum[p] + gri[p]

        @pl.when(jnp.logical_and(s == 0, here))
        def _():
            home_local(s).start()

        @pl.when(s > 0)
        def _():
            home_copy(s).start()

        @pl.when(jnp.logical_and(s == 1, r + c == 2))
        def _():
            t1.wait_recv()
            share_on.start()

        @pl.when(jnp.logical_and(s == r + 1, c == 0))
        def _():
            t2a.wait_recv()

            @pl.when(r == 0)
            def _():
                relay.wait_recv()

            share_on.start()

        @pl.when(jnp.logical_and(s == 0, r > c))
        def _():
            t2a.start()

        @pl.when(jnp.logical_and(s == 2, r < c))
        def _():
            t3.wait_recv()
            share_far.start()

        for e in range(1, E // CH):
            source_grad(e)
        left_half(theirs)
        gl_copy(s, 0).start()
        left_half(mine)

        @pl.when(jnp.logical_and(s == 0, r + c == 0))
        def _():
            t2a.start()

        @pl.when(jnp.logical_and(s == 0, jnp.logical_not(here)))
        def _():
            home_copy(0).start()

        @pl.when(s < STEPS - 1)
        def _():
            gl_copy(s, 1).start()

        @pl.when(jnp.logical_and(s == 0, r < c))
        def _():
            t1.wait_recv()
            share_on.start()

        @pl.when(jnp.logical_and(s == 0, r < c))
        def _():
            t3.start()

        @pl.when(jnp.logical_and(s == 1, here))
        def _():
            home_local(s).wait()

        @pl.when(jnp.logical_and(s == 1, jnp.logical_not(here)))
        def _():
            home_copy(0).wait_send()

        @pl.when(s > 1)
        def _():
            home_copy(s - 1).wait_send()

        gl_copy(s, 0).wait_send()
        gl_in = remote(glo.at[p, :, mine], gli.at[p, :, mine], gl_send.at[p, 0], gl_recv.at[p, 0], sibling)
        gl_in.wait_recv()

        @pl.when(s < STEPS - 1)
        def _():
            gl_copy(s, 1).wait_send()
            other = remote(glo.at[p, :, theirs], gli.at[p, :, theirs], gl_send.at[p, 1], gl_recv.at[p, 1], sibling)
            other.wait_recv()
            for c0 in range(0, CAP, 256):
                col = pl.ds(c0, 256)
                g = glo[p, :, col] + gli[p, :, col]
                v = state[:, col] + jnp.sum(g * g, axis=0, keepdims=True) * (1.0 / D)
                x = left[:, col] - LR * g / (jnp.sqrt(v[0:1]) + EPS)
                state[:, col] = v
                left[:, col] = x
                split_to(lhl, col, x)

        @pl.when(s == r + c)
        def _():
            share_on.wait_recv()

        @pl.when(jnp.logical_and(s == 2, r + c == 0))
        def _():
            share_far.wait_recv()

        return carry

    lax.fori_loop(0, STEPS, bucket, 0)

    p = (STEPS - 1) % 2
    g = glo[p, :, mine] + gli[p, :, mine]
    v = state[:, mine] + jnp.sum(g * g, axis=0, keepdims=True) * (1.0 / D)
    lfin[0] = left[:, mine] - LR * g / (jnp.sqrt(v[0:1]) + EPS)
    sfin[0] = v
    fin = remote(lfin.at[0], lfin.at[1], fin_send.at[0], fin_recv.at[0], home(0))
    fin_state = remote(sfin.at[0], sfin.at[1], fin_send.at[1], fin_recv.at[1], home(0))
    fin_here = pltpu.make_async_copy(lfin.at[0], lfin.at[1], local_sem.at[0])
    fin_state_here = pltpu.make_async_copy(sfin.at[0], sfin.at[1], local_sem.at[1])

    @pl.when(here)
    def _():
        fin_here.start()
        fin_state_here.start()

    @pl.when(jnp.logical_not(here))
    def _():
        fin.start()
        fin_state.start()
        home_copy(0).wait_recv()

    share.wait_send()
    share_state.wait_send()
    share_on.wait_send()

    @pl.when(c == 0)
    def _():
        low.wait_send()

    @pl.when(c == 1)
    def _():
        low_end.wait_send()
        t1.wait_send()

    @pl.when(c == 0)
    def _():
        t2a.wait_send()

    @pl.when(r > c)
    def _():
        t2b.wait_send()
        relay.wait_send()

    @pl.when(r < c)
    def _():
        t3.wait_send()
        share_far.wait_send()

    for s in range(1, STEPS):
        home_copy(s).wait_recv()
    total = (carr[0] + carr[1]) + (carr[2] + carr[3])

    @pl.when(here)
    def _():
        fin_here.wait()
        fin_state_here.wait()

    @pl.when(jnp.logical_not(here))
    def _():
        fin.wait()
        fin_state.wait()

    v = sfin[1] + jnp.sum(total * total, axis=0, keepdims=True) * (1.0 / D)
    out[...] = lfin[1] - LR * total / (jnp.sqrt(v[0:1]) + EPS)
    out_state[...] = v[0:1]
    home_copy(STEPS - 1).wait_send()


def train_call(blocks, ids, old, new, idx, saved, saved_state, rel, rel_end):
    dma = pltpu.SemaphoreType.DMA
    return pl.pallas_call(
        functools.partial(train_kernel, blocks),
        out_shape=(jax.ShapeDtypeStruct((D, HALF), F32), jax.ShapeDtypeStruct((1, HALF), F32)),
        in_specs=[SMEM, SMEM, SMEM, VMEM, ANY, VMEM, ANY, ANY],
        out_specs=(VMEM, VMEM),
        scratch_shapes=[
            pltpu.VMEM((D + 8, LOW), F32),
            pltpu.VMEM((D + 8, LOW), F32),
            pltpu.VMEM((5, D, CAP), F32),
            pltpu.VMEM((2, 8, CAP), F32),
            pltpu.VMEM(rel.shape[::-1], F32),
            pltpu.VMEM((2, D, E), F32),
            pltpu.VMEM((2, 128, ROWS_W), F32),
            pltpu.VMEM((D, CAP), F32),
            pltpu.VMEM((8, CAP), F32),
            pltpu.VMEM((2 * D, CAP), BF),
            pltpu.VMEM((2 * D, CAP), BF),
            pltpu.VMEM((CAP, E), BF),
            pltpu.VMEM((CAP, E + N), BF),
            pltpu.VMEM((2 * D, E), BF),
            pltpu.VMEM((2 * D, E + N), BF),
            pltpu.VMEM((D, CH), F32),
            pltpu.VMEM((D, CH), F32),
            pltpu.VMEM((D, E), F32),
            pltpu.VMEM((1, E), F32),
            pltpu.VMEM((D, E), BF),
            pltpu.VMEM((N, E), BF),
            pltpu.VMEM((2, D, CAP), F32),
            pltpu.VMEM((2, D, CAP), F32),
            pltpu.VMEM((2, D, HALF), F32),
            pltpu.VMEM((2, D, HALF), F32),
            pltpu.VMEM((2, D, HALF), F32),
            pltpu.VMEM((STEPS, D, HALF), F32),
            pltpu.VMEM((2, D, HALF), F32),
            pltpu.VMEM((2, 8, HALF), F32),
            dma((6,)),
            dma((9,)),
            dma((9,)),
            dma((2, 2)),
            dma((2, 2)),
            dma((2,)),
            dma((2,)),
            dma((2,)),
            dma((STEPS,)),
            dma((2,)),
            dma((2,)),
            dma((1,)),
            dma((1,)),
        ],
        compiler_params=pltpu.CompilerParams(
            vmem_limit_bytes=VMEM_LIMIT, collective_id=0, has_side_effects=True),
        cost_estimate=pl.CostEstimate(flops=4 * 10**10, bytes_accessed=10**7, transcendentals=0),
        name="train",
    )(ids, old, new, idx, saved, saved_state, rel, rel_end)


def local(blocks, saved_rows, saved_state, old_starts, new_starts, relations,
          source_rows, target_rows, relation_ids, negative_rows, live_groups):
    b = lax.axis_index("blk")
    r = lax.axis_index("rep")
    c = b % 2

    def move(x, route):
        pairs = []
        for m in range(blocks // 2):
            for rr in range(2):
                for cc in range(2):
                    to = route(m, rr, cc)
                    if to is not None:
                        tb, tr = to
                        pairs.append(((2 * m + cc) * 2 + rr, (tb % blocks) * 2 + tr))
        return lax.ppermute(x, BOTH, pairs)

    def sibling(x):
        return move(x, lambda m, rr, cc: (2 * m + 1 - cc, rr))

    def pad(x, fill=-1):
        return jnp.pad(x, ((0, 0), (0, E - x.shape[1])), constant_values=fill)[:, None]

    def pack(g):
        def one(x):
            return pad(lax.dynamic_index_in_dim(x[0], g, 1, keepdims=False))

        rels = pad(lax.dynamic_index_in_dim(relation_ids[0], g, 1, keepdims=False), 0)
        alive = (g < live_groups[0]).astype(jnp.int32)[:, None]
        alive = pad(jnp.broadcast_to(alive, (STEPS, source_rows.shape[3])), 0)
        parts = [one(source_rows), one(target_rows), one(negative_rows), rels, alive]
        return jnp.concatenate(parts + [jnp.zeros((STEPS, 3, E), jnp.int32)], axis=1)

    theirs = sibling(pack(1 - c))
    idx = jnp.where(c == r, pack(c), theirs)

    rel = relations.T
    end_at = rel.shape[1] // CAP * CAP
    rel_end = jnp.pad(rel[:, end_at:], ((0, 0), (0, end_at + 128 - rel.shape[1])))
    left, state = train_call(
        blocks, idx[:, 3], old_starts, new_starts, idx, saved_rows.T, saved_state[None], rel, rel_end)
    return left.T, state[0]


def solution(mesh):
    return jax.shard_map(
        functools.partial(local, mesh.shape["blk"]),
        mesh=mesh,
        in_specs=(
            P("blk", None),
            P("blk"),
            P(),
            P(),
            P(),
            P("blk", None, None, None),
            P("blk", None, None, None),
            P("blk", None, None, None),
            P("blk", None, None, None),
            P("blk", None),
        ),
        out_specs=(P(("blk", "rep"), None), P(("blk", "rep"))),
        check_vma=False,
    )
```
